32 devices in a mesh: dp: 2 (over y), tm: 4 (over x, core), height: 4 (over z).
Axes of the slice: x: 2, y: 2, z: 4, core: 2. Of those that a mesh axis runs over, the one named last changes fastest.
Arguments:
- queries: bfloat16 [2, 16, 16, 8, 2560], P('dp', 'tm', 'height'), may hold values from -9 to 9
- keys: bfloat16 [2, 16, 16, 8, 2560], P('dp', 'tm', 'height'), may hold values from -9 to 9
- values: bfloat16 [2, 16, 16, 8, 2560], P('dp', 'tm', 'height'), may hold values from -6 to 6
- projection: bfloat16 [2560, 2560], P('dp'), may hold values from -0.125 to 0.125
- d_outputs: bfloat16 [2, 16, 16, 8, 2560], P('dp', 'tm', 'height'), may hold values from -6 to 6
Outputs:
- outputs: bfloat16 [2, 16, 16, 8, 2560], P('dp', 'tm', 'height')
- d_queries: bfloat16 [2, 16, 16, 8, 2560], P('dp', 'tm', 'height')
- d_keys: bfloat16 [2, 16, 16, 8, 2560], P('dp', 'tm', 'height')
- d_values: bfloat16 [2, 16, 16, 8, 2560], P('dp', 'tm', 'height')
The draws below stay inside these ranges and needn't reach their ends.
All inputs are finite; a program needn't handle non-finite values.
Results may differ from the reference program's by a relative error of at most 0.01.
Values may be sent and summed in bfloat16 or wider, within the bound.
A program may use at most 128 MiB of HBM per device.

```python
import math
import jax
import jax.numpy as jnp
from jax import lax

HEADS = 20
HDIM = 128
DW = 2560
TILE = 2
TWIDE = 4
TILES_W = 2
VIDEOS = 2
FRAMES = 16
ROWS = 16
COLS = 8
QKDIM = 2560
N_TM = 4
N_HEIGHT = 4


def drawn_pair(key):
    seeded = jax.random.fold_in(key, 4111)
    seed_query, seed_key = jax.random.split(seeded, 2)
    full_shape = (VIDEOS, FRAMES, ROWS, COLS, HEADS, HDIM)
    merged_shape = (VIDEOS, FRAMES, ROWS, COLS, HEADS * HDIM)
    query_part = jax.random.truncated_normal(seed_query, -6.0, 6.0, full_shape, jnp.float32).reshape(merged_shape)
    key_part = jax.random.truncated_normal(seed_key, -6.0, 6.0, full_shape, jnp.float32).reshape(merged_shape)
    return (query_part.astype(jnp.bfloat16), key_part.astype(jnp.bfloat16))


def draw_queries(key, part):
    return drawn_pair(key)[0]


def draw_keys(key, part):
    return drawn_pair(key)[1]


def shard_levels(stream_key, extent, shards, smallest, high):
    level, own = 1.0, jax.random.fold_in(stream_key, 6)
    for position, blocks in shards:
        heights = jnp.exp(jax.random.uniform(jax.random.fold_in(own, position), (blocks,), jnp.float32, smallest / len(shards), high / len(shards)))
        level = level * jnp.repeat(heights, extent[position] // blocks).reshape([-1 if axis == position else 1 for axis in range(len(extent))])
    return level


def noise(stream_key, dims, width, reach, shards=(), kind=jnp.bfloat16):
    array = jax.random.normal(stream_key, dims, jnp.float32) * width
    if len(shards) > 0:
        array = shard_levels(stream_key, dims, shards, -0.22, 0.18) * array
    return jnp.clip(array, min=-reach, max=reach).astype(kind)


def setup_inputs(seed: int = 0) -> dict:
    key_list = jax.random.split(jax.random.key(seed), 6)
    return {
        "queries": draw_queries(jax.random.fold_in(key_list[5], 71), 0),
        "keys": draw_keys(jax.random.fold_in(key_list[5], 71), 0),
        "values": noise(key_list[2], (VIDEOS, FRAMES, ROWS, COLS, QKDIM), 1.0, 6.0, ((0, 2), (1, 4), (2, 4))),
        "projection": noise(key_list[3], (QKDIM, DW), QKDIM ** -0.5, 0.125, ((0, 2),)),
        "d_outputs": noise(key_list[4], (VIDEOS, FRAMES, ROWS, COLS, DW), 1.0, 6.0, ((0, 2), (1, 4), (2, 4))),
    }


def window_mask(frame_block, row_block, frame_blocks, row_blocks, tiles_across, tile_len, tile_cols):
    grid_shape = (2, 2, tiles_across, 4, 4, tiles_across)
    query_frame = lax.broadcasted_iota(jnp.int32, grid_shape, 0)
    query_row = lax.broadcasted_iota(jnp.int32, grid_shape, 1)
    query_column = lax.broadcasted_iota(jnp.int32, grid_shape, 2)
    key_frame = lax.broadcasted_iota(jnp.int32, grid_shape, 3)
    key_row = lax.broadcasted_iota(jnp.int32, grid_shape, 4)
    key_column = lax.broadcasted_iota(jnp.int32, grid_shape, 5)
    frame_step = key_frame - query_frame - 1
    row_step = key_row - query_row - 1
    column_step = key_column - query_column
    frame_tile = 2 * frame_block + key_frame - 1
    row_tile = 2 * row_block + key_row - 1
    inside = (jnp.abs(frame_step) <= 1) & (jnp.abs(row_step) <= 1) & (jnp.abs(column_step) <= 1)
    inside = inside & (frame_tile >= 0) & (frame_tile < 2 * frame_blocks)
    inside = inside & (row_tile >= 0) & (row_tile < 2 * row_blocks)
    spread = inside[:, None, :, None, :, None, :, None, :, None, :, None]
    spread = jnp.broadcast_to(spread, (2, tile_len, 2, tile_len, tiles_across, tile_cols, 4, tile_len, 4, tile_len, tiles_across, tile_cols))
    query_count = 4 * tile_len * tile_len * tiles_across * tile_cols
    return spread.reshape(query_count, 4 * query_count)

def attend_forward(query_block, key_ext, value_ext, window):
    query_count = window.shape[0]
    key_count = window.shape[1]
    query_heads = query_block.reshape(query_count, HEADS, HDIM).astype(jnp.float32)
    key_heads = key_ext.reshape(key_count, HEADS, HDIM).astype(jnp.float32)
    value_heads = value_ext.reshape(key_count, HEADS, HDIM).astype(jnp.float32)
    scaling = 1.0 / math.sqrt(HDIM)
    scores = jnp.einsum('qhd,khd->hqk', query_heads, key_heads) * scaling
    masked = jnp.where(window[None], scores, -jnp.inf)
    largest = lax.optimization_barrier(jnp.max(masked, axis=2, keepdims=True))
    weights = jnp.exp(masked - largest)
    soft_weights = (weights / lax.optimization_barrier(jnp.sum(weights, axis=2, keepdims=True))).astype(jnp.bfloat16)
    soft_weights = lax.optimization_barrier(soft_weights)
    attended = jnp.einsum('hqk,khd->qhd', soft_weights.astype(jnp.float32), value_heads)
    return (attended.reshape(query_count, HEADS * HDIM).astype(jnp.bfloat16), soft_weights)

def attend_backward(query_block, key_ext, value_ext, soft_weights, grad_attended):
    query_count = soft_weights.shape[1]
    key_count = soft_weights.shape[2]
    query_heads = query_block.reshape(query_count, HEADS, HDIM).astype(jnp.float32)
    key_heads = key_ext.reshape(key_count, HEADS, HDIM).astype(jnp.float32)
    value_heads = value_ext.reshape(key_count, HEADS, HDIM).astype(jnp.float32)
    grad_heads = grad_attended.reshape(query_count, HEADS, HDIM).astype(jnp.float32)
    scaling = 1.0 / math.sqrt(HDIM)
    weights_wide = soft_weights.astype(jnp.float32)
    grad_weights = jnp.einsum('qhd,khd->hqk', grad_heads, value_heads)
    row_dot = lax.optimization_barrier(jnp.sum(weights_wide * grad_weights, axis=2, keepdims=True))
    grad_scores = (weights_wide * (grad_weights - row_dot) * scaling).astype(jnp.bfloat16)
    grad_scores = lax.optimization_barrier(grad_scores).astype(jnp.float32)
    grad_query = jnp.einsum('hqk,khd->qhd', grad_scores, key_heads).reshape(query_count, HEADS * HDIM).astype(jnp.bfloat16)
    grad_key = jnp.einsum('hqk,qhd->khd', grad_scores, query_heads).reshape(key_count, HEADS * HDIM)
    grad_value = jnp.einsum('hqk,qhd->khd', weights_wide, grad_heads).reshape(key_count, HEADS * HDIM)
    return (grad_query, grad_key, grad_value)

def one_video(operands, projection):
    query_video, key_video, value_video, cotangent = operands
    side = 2 * TILE
    pad_spec = ((TILE, TILE), (TILE, TILE), (0, 0), (0, 0))
    key_padded = jnp.pad(key_video, pad_spec)
    value_padded = jnp.pad(value_video, pad_spec)
    block_count = N_TM * N_HEIGHT
    anchor = jnp.zeros((), jnp.int32)

    def block_slices(index):
        index = index.astype(jnp.int32)
        frame_block = index // N_HEIGHT
        row_block = index % N_HEIGHT
        query_block = lax.dynamic_slice(query_video, (frame_block * side, row_block * side, anchor, anchor), (side, side, COLS, QKDIM))
        key_ext = lax.dynamic_slice(key_padded, (frame_block * side, row_block * side, anchor, anchor), (2 * side, 2 * side, COLS, QKDIM))
        value_ext = lax.dynamic_slice(value_padded, (frame_block * side, row_block * side, anchor, anchor), (2 * side, 2 * side, COLS, QKDIM))
        window = window_mask(frame_block, row_block, N_TM, N_HEIGHT, TILES_W, TILE, TWIDE)
        return (query_block, key_ext, value_ext, window)

    def forward_block(index):
        query_block, key_ext, value_ext, window = block_slices(index)
        return attend_forward(query_block, key_ext, value_ext, window)
    block_ids = jnp.arange(block_count, dtype=jnp.int32)
    attended_blocks, weight_blocks = lax.map(forward_block, block_ids)
    attended = attended_blocks.reshape(N_TM, N_HEIGHT, side, side, COLS, QKDIM).transpose(0, 2, 1, 3, 4, 5)
    attended = attended.reshape(FRAMES * ROWS * COLS, QKDIM)
    outputs = jnp.dot(attended, projection, preferred_element_type=jnp.float32).astype(jnp.bfloat16)
    grad_attended = jnp.dot(cotangent.reshape(FRAMES * ROWS * COLS, DW), projection.T, preferred_element_type=jnp.float32).astype(jnp.bfloat16)
    grad_blocks = grad_attended.reshape(N_TM, side, N_HEIGHT, side, COLS, QKDIM).transpose(0, 2, 1, 3, 4, 5)
    grad_blocks = grad_blocks.reshape(block_count, side * side * COLS, QKDIM)

    def backward_block(block_items):
        index, soft_weights, grad_block = block_items
        query_block, key_ext, value_ext, window = block_slices(index)
        grad_query, grad_key, grad_value = attend_backward(query_block, key_ext, value_ext, soft_weights, grad_block)
        stacked = jnp.stack((grad_key, grad_value)).reshape(2, 2 * side, 2 * side, COLS, QKDIM)
        frame_pos = lax.broadcasted_iota(jnp.int32, stacked.shape, 1)
        row_pos = lax.broadcasted_iota(jnp.int32, stacked.shape, 2)
        center = (frame_pos >= TILE) & (frame_pos < 3 * TILE) & (row_pos >= TILE) & (row_pos < 3 * TILE)
        rounded = lax.optimization_barrier(stacked.astype(jnp.bfloat16)).astype(jnp.float32)
        return (grad_query, jnp.where(center, stacked, rounded))
    query_grads, partials = lax.map(backward_block, (block_ids, weight_blocks, grad_blocks))

    def add_block(index, running):
        index = index.astype(jnp.int32)
        frame_block = index // N_HEIGHT
        row_block = index % N_HEIGHT
        start = (anchor, frame_block * side, row_block * side, anchor, anchor)
        current = lax.dynamic_slice(running, start, (2, 2 * side, 2 * side, COLS, QKDIM))
        return lax.dynamic_update_slice(running, current + partials[index], start)
    running = jnp.zeros((2, FRAMES + 2 * TILE, ROWS + 2 * TILE, COLS, QKDIM), jnp.float32)
    running = lax.fori_loop(0, block_count, add_block, running)
    gradients = running[:, TILE:TILE + FRAMES, TILE:TILE + ROWS].astype(jnp.bfloat16)
    d_queries = query_grads.reshape(N_TM, N_HEIGHT, side, side, COLS, QKDIM).transpose(0, 2, 1, 3, 4, 5)
    d_queries = d_queries.reshape(FRAMES, ROWS, COLS, QKDIM)
    return (outputs.reshape(FRAMES, ROWS, COLS, DW), d_queries, gradients[0], gradients[1])

def reference(queries, keys, values, projection, d_outputs):

    def per_video(operands):
        return one_video(operands, projection)
    return lax.map(per_video, (queries, keys, values, d_outputs))
```

```python
import functools
import math

import jax
import jax.numpy as jnp
import numpy as np
from jax import lax
from jax.experimental import pallas as pl
from jax.experimental.pallas import tpu as pltpu
from jax.sharding import PartitionSpec as P

HEADS = 20
HDIM = 128
TWIDE = 4
TILES_W = 2

FAR = -1e30


def key_tiles():
    own, low, high = (1, 2), (0,), (3,)
    return (
        (own, own),
        (own, low),
        (own, high),
        (low, own),
        (high, own),
        (low, low),
        (low, high),
        (high, low),
        (high, high),
    )


def tile_coords(tile_len, cols):
    frames, rows = [], []
    for frame_tiles, row_tiles in key_tiles():
        f = np.repeat(np.array(frame_tiles), tile_len)
        r = np.repeat(np.array(row_tiles), tile_len)
        frames.append(np.broadcast_to(f[:, None, None], (len(f), len(r), cols)).reshape(-1))
        rows.append(np.broadcast_to(r[None, :, None], (len(f), len(r), cols)).reshape(-1))
    return np.concatenate(frames), np.concatenate(rows)


def window_bias(tile_len, cols, tile_cols):
    frames, rows = tile_coords(tile_len, cols)
    query_count = 4 * tile_len * tile_len * cols
    query_frames, query_rows = frames[:query_count], rows[:query_count]
    column_tiles = np.arange(cols) // tile_cols
    key_columns = np.tile(column_tiles, len(frames) // cols)
    query_columns = np.tile(column_tiles, query_count // cols)
    inside = np.abs(frames[:, None] - query_frames[None]) <= 1
    inside &= np.abs(rows[:, None] - query_rows[None]) <= 1
    inside &= np.abs(key_columns[:, None] - query_columns[None]) <= 1
    frame_block, frame_blocks = lax.axis_index("tm"), lax.axis_size("tm")
    row_block, row_blocks = lax.axis_index("height"), lax.axis_size("height")
    frame_tile = 2 * frame_block + jnp.asarray(frames, jnp.int32)[:, None] - 1
    row_tile = 2 * row_block + jnp.asarray(rows, jnp.int32)[:, None] - 1
    present = (frame_tile >= 0) & (frame_tile < 2 * frame_blocks)
    present = present & (row_tile >= 0) & (row_tile < 2 * row_blocks)
    return jnp.where(present & jnp.asarray(inside), 0.0, FAR).astype(jnp.float32)


def rows_of(value):
    return value.astype(jnp.float32).reshape(-1, value.shape[-1]).astype(jnp.bfloat16)


def attention_kernel(
    heads,
    scaling,
    bias_ref,
    q_ref,
    k_ref,
    v_ref,
    top_ref,
    bottom_ref,
    left_ref,
    right_ref,
    corner_left_ref,
    corner_right_ref,
    da_ref,
    att_ref,
    dq_ref,
    d_own_ref,
    d_top_ref,
    d_bottom_ref,
    d_left_ref,
    d_right_ref,
    d_corner_left_ref,
    d_corner_right_ref,
):
    f32 = jnp.float32

    def gather(which, own_ref, cols):
        parts = [rows_of(own_ref[:, :, :, cols])]
        for ref in (top_ref, bottom_ref, left_ref, right_ref):
            parts.append(rows_of(ref[which, :, :, :, cols]))
        for ref in (corner_left_ref, corner_right_ref):
            for side in range(2):
                parts.append(rows_of(ref[which, side, :, :, :, cols]))
        return jnp.concatenate(parts, axis=0)

    def scatter(which, grads, cols):
        start = 0
        for ref in (d_own_ref, d_top_ref, d_bottom_ref, d_left_ref, d_right_ref):
            shape = ref.shape[1:-1] + (HDIM,)
            count = shape[0] * shape[1] * shape[2]
            part = grads[start : start + count].reshape(shape)
            ref[which, :, :, :, cols] = part.astype(ref.dtype)
            start += count
        for ref in (d_corner_left_ref, d_corner_right_ref):
            shape = ref.shape[2:-1] + (HDIM,)
            count = shape[0] * shape[1] * shape[2]
            for side in range(2):
                part = grads[start : start + count].reshape(shape)
                ref[which, side, :, :, :, cols] = part.astype(ref.dtype)
                start += count

    for head in range(heads):
        cols = slice(head * HDIM, (head + 1) * HDIM)
        q = rows_of(q_ref[:, :, :, cols])
        k = gather(0, k_ref, cols)
        v = gather(1, v_ref, cols)
        da = da_ref[:, cols]
        scores = lax.dot_general(k, q, (((1,), (1,)), ((), ())), preferred_element_type=f32)
        scores = scores * scaling + bias_ref[...]
        largest = jnp.max(scores, axis=0, keepdims=True)
        weights = jnp.exp(scores - largest)
        inverse = 1.0 / jnp.sum(weights, axis=0, keepdims=True)
        probs = (weights * inverse).astype(jnp.bfloat16)
        att = lax.dot_general(probs, v, (((0,), (0,)), ((), ())), preferred_element_type=f32)
        att_ref[:, cols] = att.astype(att_ref.dtype)
        wide = probs.astype(f32)
        d_probs = lax.dot_general(v, da, (((1,), (1,)), ((), ())), preferred_element_type=f32)
        row_dot = jnp.sum(wide * d_probs, axis=0, keepdims=True)
        d_scores = (wide * (d_probs - row_dot) * scaling).astype(jnp.bfloat16)
        dq = lax.dot_general(d_scores, k, (((0,), (0,)), ((), ())), preferred_element_type=f32)
        shape = dq_ref.shape[:-1] + (HDIM,)
        dq_ref[:, :, :, cols] = dq.reshape(shape).astype(dq_ref.dtype)
        scatter(0, jnp.dot(d_scores, q, preferred_element_type=f32), cols)
        scatter(1, jnp.dot(probs, da, preferred_element_type=f32), cols)


def attention(bias, q, k, v, pieces, da):
    width = 2 * HDIM if HEADS % 2 == 0 else HDIM
    dim = q.shape[-1]

    def blocked(array):
        lead = array.ndim - 1
        return pl.BlockSpec(array.shape[:-1] + (width,), lambda i: (0,) * lead + (i,))

    operands = (q, k, v, *pieces, da)
    grads = [jax.ShapeDtypeStruct((2,) + k.shape, jnp.float32)]
    grads += [jax.ShapeDtypeStruct(p.shape, jnp.bfloat16) for p in pieces]
    outs = [jax.ShapeDtypeStruct(da.shape, jnp.bfloat16), jax.ShapeDtypeStruct(q.shape, q.dtype)]
    outs += grads
    keys, queries = bias.shape
    moved = 2 * sum(math.prod(a.shape) for a in operands + tuple(outs))
    return pl.pallas_call(
        functools.partial(attention_kernel, width // HDIM, 1.0 / math.sqrt(HDIM)),
        grid=(dim // width,),
        out_shape=outs,
        in_specs=[pl.BlockSpec(bias.shape, lambda i: (0, 0))] + [blocked(a) for a in operands],
        out_specs=[blocked(o) for o in outs],
        compiler_params=pltpu.CompilerParams(vmem_limit_bytes=40 * 1024 * 1024),
        cost_estimate=pl.CostEstimate(
            flops=12 * keys * queries * dim,
            bytes_accessed=moved,
            transcendentals=keys * queries * dim // HDIM,
        ),
        name="attention",
    )(bias, *operands)


def shifted(array, axis, step):
    count = lax.axis_size(axis)
    pairs = [(i, i + step) for i in range(count) if 0 <= i + step < count]
    return lax.ppermute(array, axis, pairs)


def rotated(array, axis, step):
    count = lax.axis_size(axis)
    return lax.ppermute(array, axis, [(i, (i + step) % count) for i in range(count)])


def contract(x, weight, weight_axis):
    return lax.dot_general(
        x, weight, (((1,), (weight_axis,)), ((), ())), preferred_element_type=jnp.float32
    )


def body(queries, keys, values, projection, d_outputs):
    f32, bf16 = jnp.float32, jnp.bfloat16
    q, k, v = queries[0], keys[0], values[0]
    frames, rows, cols, dim = q.shape
    tile_len = frames // 2
    query_count = frames * rows * cols
    depth = projection.shape[0]
    dp_count, dp_index = lax.axis_size("dp"), lax.axis_index("dp")

    low_rows = jnp.stack((k[:, :tile_len], v[:, :tile_len]))
    high_rows = jnp.stack((k[:, tile_len:], v[:, tile_len:]))
    low_frames = jnp.stack((k[:tile_len], v[:tile_len]))
    high_frames = jnp.stack((k[tile_len:], v[tile_len:]))
    top = shifted(high_rows, "height", 1)
    bottom = shifted(low_rows, "height", -1)
    left = shifted(high_frames, "tm", 1)
    right = shifted(low_frames, "tm", -1)
    corner_left = shifted(jnp.stack((top[:, tile_len:], bottom[:, tile_len:]), 1), "tm", 1)
    corner_right = shifted(jnp.stack((top[:, :tile_len], bottom[:, :tile_len]), 1), "tm", -1)

    cotangent = d_outputs.reshape(query_count, d_outputs.shape[-1])
    d_attended = jnp.zeros((query_count, dim), bf16)
    for step in range(dp_count):
        x = rotated(cotangent, "dp", step) if step else cotangent
        part = contract(x, projection, 1).astype(bf16)
        part = rotated(part, "dp", -step) if step else part
        owner = lax.rem(dp_index + step, dp_count)
        d_attended = lax.dynamic_update_slice_in_dim(d_attended, part, owner * depth, 1)

    bias = window_bias(tile_len, cols, TWIDE)
    pieces = (top, bottom, left, right, corner_left, corner_right)
    attended, d_queries, d_own, *d_pieces = attention(bias, q, k, v, pieces, d_attended)
    d_top, d_bottom, d_left, d_right, d_corner_left, d_corner_right = d_pieces

    corners_high = shifted(d_corner_left, "tm", -1)
    corners_low = shifted(d_corner_right, "tm", 1)
    corners = jnp.concatenate((corners_low, corners_high), axis=2).astype(f32)
    to_top = (d_top.astype(f32) + corners[:, 0]).astype(bf16)
    to_bottom = (d_bottom.astype(f32) + corners[:, 1]).astype(bf16)
    from_bottom = shifted(to_top, "height", -1)
    from_top = shifted(to_bottom, "height", 1)
    from_right = shifted(d_left, "tm", -1)
    from_left = shifted(d_right, "tm", 1)
    summed = d_own + jnp.concatenate((from_left, from_right), axis=1).astype(f32)
    summed = summed + jnp.concatenate((from_top, from_bottom), axis=2).astype(f32)
    summed = summed.astype(bf16)

    outputs = None
    for step in range(dp_count):
        owner = lax.rem(dp_index + step, dp_count)
        x = lax.dynamic_slice_in_dim(attended, owner * depth, depth, 1)
        x = rotated(x, "dp", step) if step else x
        part = contract(x, projection, 0)
        part = rotated(part.astype(bf16), "dp", -step).astype(f32) if step else part
        outputs = part if outputs is None else outputs + part
    outputs = outputs.astype(bf16)
    return (
        outputs.reshape(d_outputs.shape),
        d_queries[None],
        summed[0][None],
        summed[1][None],
    )


def solution(mesh):
    spread = P("dp", "tm", "height", None, None)
    in_specs = (spread, spread, spread, P("dp", None), spread)
    return jax.shard_map(
        body, mesh=mesh, in_specs=in_specs, out_specs=(spread,) * 4, check_vma=False
    )
```

```python
import functools
import math

import jax
import jax.numpy as jnp
import numpy as np
from jax import lax
from jax.experimental import pallas as pl
from jax.experimental.pallas import tpu as pltpu
from jax.sharding import PartitionSpec as P

HEADS = 20
HDIM = 128
TWIDE = 4
TILES_W = 2

FAR = -1e30


def key_tiles():
    own, low, high = (1, 2), (0,), (3,)
    return (
        (own, own),
        (own, low),
        (own, high),
        (low, own),
        (high, own),
        (low, low),
        (low, high),
        (high, low),
        (high, high),
    )


def tile_coords(tile_len, cols):
    frames, rows = [], []
    for frame_tiles, row_tiles in key_tiles():
        f = np.repeat(np.array(frame_tiles), tile_len)
        r = np.repeat(np.array(row_tiles), tile_len)
        frames.append(np.broadcast_to(f[:, None, None], (len(f), len(r), cols)).reshape(-1))
        rows.append(np.broadcast_to(r[None, :, None], (len(f), len(r), cols)).reshape(-1))
    return np.concatenate(frames), np.concatenate(rows)


def window_bias(tile_len, cols, tile_cols):
    frames, rows = tile_coords(tile_len, cols)
    query_count = 4 * tile_len * tile_len * cols
    query_frames, query_rows = frames[:query_count], rows[:query_count]
    column_tiles = np.arange(cols) // tile_cols
    key_columns = np.tile(column_tiles, len(frames) // cols)
    query_columns = np.tile(column_tiles, query_count // cols)
    inside = np.abs(frames[:, None] - query_frames[None]) <= 1
    inside &= np.abs(rows[:, None] - query_rows[None]) <= 1
    inside &= np.abs(key_columns[:, None] - query_columns[None]) <= 1
    frame_block, frame_blocks = lax.axis_index("tm"), lax.axis_size("tm")
    row_block, row_blocks = lax.axis_index("height"), lax.axis_size("height")
    frame_tile = 2 * frame_block + jnp.asarray(frames, jnp.int32)[:, None] - 1
    row_tile = 2 * row_block + jnp.asarray(rows, jnp.int32)[:, None] - 1
    present = (frame_tile >= 0) & (frame_tile < 2 * frame_blocks)
    present = present & (row_tile >= 0) & (row_tile < 2 * row_blocks)
    return jnp.where(present & jnp.asarray(inside), 0.0, FAR).astype(jnp.float32)


def rows_of(value):
    return value.astype(jnp.float32).reshape(-1, value.shape[-1]).astype(jnp.bfloat16)


def attention_kernel(
    heads,
    scaling,
    bias_ref,
    q_ref,
    k_ref,
    v_ref,
    top_ref,
    bottom_ref,
    left_ref,
    right_ref,
    corner_left_ref,
    corner_right_ref,
    da_ref,
    att_ref,
    dq_ref,
    d_own_ref,
    d_top_ref,
    d_bottom_ref,
    d_left_ref,
    d_right_ref,
    d_corner_left_ref,
    d_corner_right_ref,
):
    f32 = jnp.float32

    def gather(which, own_ref, cols):
        parts = [rows_of(own_ref[:, :, :, cols])]
        for ref in (top_ref, bottom_ref, left_ref, right_ref):
            parts.append(rows_of(ref[which, :, :, :, cols]))
        for ref in (corner_left_ref, corner_right_ref):
            for side in range(2):
                parts.append(rows_of(ref[which, side, :, :, :, cols]))
        return jnp.concatenate(parts, axis=0)

    def scatter(which, grads, cols):
        start = 0
        for ref in (d_own_ref, d_top_ref, d_bottom_ref, d_left_ref, d_right_ref):
            shape = ref.shape[1:-1] + (HDIM,)
            count = shape[0] * shape[1] * shape[2]
            part = grads[start : start + count].reshape(shape)
            ref[which, :, :, :, cols] = part.astype(ref.dtype)
            start += count
        for ref in (d_corner_left_ref, d_corner_right_ref):
            shape = ref.shape[2:-1] + (HDIM,)
            count = shape[0] * shape[1] * shape[2]
            for side in range(2):
                part = grads[start : start + count].reshape(shape)
                ref[which, side, :, :, :, cols] = part.astype(ref.dtype)
                start += count

    for head in range(heads):
        cols = slice(head * HDIM, (head + 1) * HDIM)
        q = rows_of(q_ref[:, :, :, cols])
        k = gather(0, k_ref, cols)
        v = gather(1, v_ref, cols)
        da = da_ref[:, cols]
        scores = lax.dot_general(k, q, (((1,), (1,)), ((), ())), preferred_element_type=f32)
        scores = scores * scaling + bias_ref[...]
        largest = jnp.max(scores, axis=0, keepdims=True)
        weights = jnp.exp(scores - largest)
        inverse = 1.0 / jnp.sum(weights, axis=0, keepdims=True)
        probs = (weights * inverse).astype(jnp.bfloat16)
        att = lax.dot_general(probs, v, (((0,), (0,)), ((), ())), preferred_element_type=f32)
        att_ref[:, cols] = att.astype(att_ref.dtype)
        wide = probs.astype(f32)
        d_probs = lax.dot_general(v, da, (((1,), (1,)), ((), ())), preferred_element_type=f32)
        row_dot = jnp.sum(wide * d_probs, axis=0, keepdims=True)
        d_scores = (wide * (d_probs - row_dot) * scaling).astype(jnp.bfloat16)
        dq = lax.dot_general(d_scores, k, (((0,), (0,)), ((), ())), preferred_element_type=f32)
        shape = dq_ref.shape[:-1] + (HDIM,)
        dq_ref[:, :, :, cols] = dq.reshape(shape).astype(dq_ref.dtype)
        scatter(0, jnp.dot(d_scores, q, preferred_element_type=f32), cols)
        scatter(1, jnp.dot(probs, da, preferred_element_type=f32), cols)


def attention(bias, q, k, v, pieces, da):
    width = 2 * HDIM if HEADS % 2 == 0 else HDIM
    dim = q.shape[-1]

    def blocked(array):
        lead = array.ndim - 1
        return pl.BlockSpec(array.shape[:-1] + (width,), lambda i: (0,) * lead + (i,))

    operands = (q, k, v, *pieces, da)
    grads = [jax.ShapeDtypeStruct((2,) + k.shape, jnp.float32)]
    grads += [jax.ShapeDtypeStruct(p.shape, jnp.bfloat16) for p in pieces]
    outs = [jax.ShapeDtypeStruct(da.shape, jnp.bfloat16), jax.ShapeDtypeStruct(q.shape, q.dtype)]
    outs += grads
    keys, queries = bias.shape
    moved = 2 * sum(math.prod(a.shape) for a in operands + tuple(outs))
    return pl.pallas_call(
        functools.partial(attention_kernel, width // HDIM, 1.0 / math.sqrt(HDIM)),
        grid=(dim // width,),
        out_shape=outs,
        in_specs=[pl.BlockSpec(bias.shape, lambda i: (0, 0))] + [blocked(a) for a in operands],
        out_specs=[blocked(o) for o in outs],
        compiler_params=pltpu.CompilerParams(vmem_limit_bytes=40 * 1024 * 1024),
        cost_estimate=pl.CostEstimate(
            flops=12 * keys * queries * dim,
            bytes_accessed=moved,
            transcendentals=keys * queries * dim // HDIM,
        ),
        name="attention",
    )(bias, *operands)


MESH = pl.DeviceIdType.MESH


class Shift:
    def __init__(self, src, dst, send, recv, axis, step):
        count, index = lax.axis_size(axis), lax.axis_index(axis)
        self.has_target = (index + step >= 0) & (index + step < count)
        self.has_source = (index - step >= 0) & (index - step < count)
        target = lax.rem(index + step + count, count)
        self.copy = pltpu.make_async_remote_copy(
            src_ref=src,
            dst_ref=dst,
            send_sem=send,
            recv_sem=recv,
            device_id={axis: target},
            device_id_type=MESH,
        )

    def start(self):
        pl.when(self.has_target)(self.copy.start)

    def wait_recv(self):
        pl.when(self.has_source)(self.copy.wait_recv)

    def wait_send(self):
        pl.when(self.has_target)(self.copy.wait_send)


def rotation(src, dst, send, recv, axis, step):
    count, index = lax.axis_size(axis), lax.axis_index(axis)
    target = lax.rem(index + step + count, count)
    return pltpu.make_async_remote_copy(
        src_ref=src,
        dst_ref=dst,
        send_sem=send,
        recv_sem=recv,
        device_id={axis: target},
        device_id_type=MESH,
    )


def greet():
    barrier = pltpu.get_barrier_semaphore()
    expected = 0
    for axis in ("tm", "height"):
        count, index = lax.axis_size(axis), lax.axis_index(axis)
        for step in (-1, 1):
            there = (index + step >= 0) & (index + step < count)
            target = lax.rem(index + step + count, count)

            @pl.when(there)
            def _(axis=axis, target=target):
                pl.semaphore_signal(
                    barrier, inc=1, device_id={axis: target}, device_id_type=MESH
                )

            expected = expected + jnp.where(there, 1, 0)
    count, index = lax.axis_size("dp"), lax.axis_index("dp")
    for step in range(1, count):
        target = lax.rem(index + step, count)
        pl.semaphore_signal(barrier, inc=1, device_id={"dp": target}, device_id_type=MESH)
    pl.semaphore_wait(barrier, expected + (count - 1))


def tiles_of(width):
    tile = 2 * HDIM if width % (2 * HDIM) == 0 else width
    return [slice(i, i + tile) for i in range(0, width, tile)]


def contract(x, weight, weight_axis):
    return lax.dot_general(
        x, weight, (((1,), (weight_axis,)), ((), ())), preferred_element_type=jnp.float32
    )


def fetch_kernel(
    k_ref,
    v_ref,
    x_ref,
    w_ref,
    top_ref,
    bottom_ref,
    left_ref,
    right_ref,
    corner_left_ref,
    corner_right_ref,
    parts_ref,
    w_held,
    x_held,
    x_arrived,
    part_held,
    send_sem,
    recv_sem,
    local_sem,
    x_send,
    x_recv,
    part_send,
    part_recv,
):
    dp_count = lax.axis_size("dp")
    half = k_ref.shape[0] // 2
    greet()
    first, filled = [], []

    def shift(src, dst, filler, axis, step, into):
        t = len(first) + (0 if into is first else len(into))
        move = Shift(src, dst, send_sem.at[t], recv_sem.at[t], axis, step)
        fill = pltpu.make_async_copy(filler, dst, local_sem.at[t])
        move.start()
        pl.when(jnp.logical_not(move.has_source))(fill.start)
        into.append((move, fill))

    for which, ref in enumerate((k_ref, v_ref)):
        low, high = ref.at[:, :half], ref.at[:, half:]
        shift(high, top_ref.at[which], high, "height", 1, first)
        shift(low, bottom_ref.at[which], low, "height", -1, first)
    exchange = []
    for step in range(1, dp_count):
        s = step - 1
        move = rotation(x_ref, x_arrived.at[s], x_send.at[s], x_recv.at[s], "dp", step)
        move.start()
        exchange.append(move)
    for which, ref in enumerate((k_ref, v_ref)):
        low, high = ref.at[:half], ref.at[half:]
        shift(high, left_ref.at[which], high, "tm", 1, first)
        shift(low, right_ref.at[which], low, "tm", -1, first)
    load_w = pltpu.make_async_copy(w_ref, w_held, local_sem.at[12])
    load_x = pltpu.make_async_copy(x_ref, x_held, local_sem.at[13])
    load_x.start()
    load_w.start()
    load_x.wait()
    load_w.wait()

    def multiply(block, slot):
        x = rows_of(block)
        for tile in tiles_of(w_held.shape[0]):
            part_held[slot, :, tile] = contract(x, w_held[tile, :], 1).astype(part_held.dtype)

    multiply(x_held[...], 0)
    keep = pltpu.make_async_copy(part_held.at[0], parts_ref.at[0], local_sem.at[14])
    keep.start()
    returned = []
    for step in range(1, dp_count):
        s = step - 1
        exchange[s].wait_recv()
        multiply(x_arrived[s], step)
        move = rotation(
            part_held.at[step], parts_ref.at[step], part_send.at[s], part_recv.at[s], "dp", -step
        )
        move.start()
        returned.append(move)

    def settle(move, fill):
        move.wait_recv()
        pl.when(jnp.logical_not(move.has_source))(fill.wait)

    second = []
    for move, fill in first[:4]:
        settle(move, fill)
    for side, ref in enumerate((top_ref, bottom_ref)):
        low, high = ref.at[:, :half], ref.at[:, half:]
        shift(high, corner_left_ref.at[:, side], high, "tm", 1, second)
        shift(low, corner_right_ref.at[:, side], low, "tm", -1, second)
    for move, fill in first[4:] + second:
        settle(move, fill)
    for move, _ in first + second:
        move.wait_send()
    for move in exchange:
        move.wait_send()
    for move in returned:
        move.wait()
    keep.wait()


def fetch(k, v, x, w):
    half = k.shape[0] // 2
    frames, rows, cols, dim = k.shape
    others = lax.axis_size("dp") - 1
    count = frames * rows * cols
    bf16 = jnp.bfloat16
    dma = pltpu.SemaphoreType.DMA
    shapes = [(2, frames, half, cols, dim)] * 2 + [(2, half, rows, cols, dim)] * 2
    shapes += [(2, 2, half, half, cols, dim)] * 2 + [(others + 1, count, w.shape[0])]
    anywhere = pl.BlockSpec(memory_space=pl.ANY)
    slots = max(others, 1)
    return pl.pallas_call(
        fetch_kernel,
        out_shape=[jax.ShapeDtypeStruct(s, bf16) for s in shapes],
        in_specs=[anywhere] * 4,
        out_specs=[anywhere] * len(shapes),
        scratch_shapes=[
            pltpu.VMEM(w.shape, bf16),
            pltpu.VMEM(x.shape, bf16),
            pltpu.VMEM((slots,) + x.shape, bf16),
            pltpu.VMEM((others + 1, count, w.shape[0]), bf16),
            dma((12,)),
            dma((12,)),
            dma((15,)),
        ]
        + [dma((slots,))] * 4,
        compiler_params=pltpu.CompilerParams(
            collective_id=0, has_side_effects=True, vmem_limit_bytes=48 * 1024 * 1024
        ),
        name="fetch",
    )(k, v, x, w)


def give_kernel(
    x_ref,
    w_ref,
    d_top_ref,
    d_bottom_ref,
    d_left_ref,
    d_right_ref,
    d_corner_left_ref,
    d_corner_right_ref,
    own_ref,
    arrived_ref,
    from_top_ref,
    from_bottom_ref,
    from_left_ref,
    from_right_ref,
    w_held,
    x_held,
    x_arrived,
    y_held,
    corners_low,
    corners_high,
    to_top,
    to_bottom,
    send_sem,
    recv_sem,
    local_sem,
    x_send,
    x_recv,
    y_send,
    y_recv,
):
    dp_count = lax.axis_size("dp")
    half = d_left_ref.shape[1]
    f32 = jnp.float32
    greet()

    def shift(src, dst, t, axis, step):
        move = Shift(src, dst, send_sem.at[t], recv_sem.at[t], axis, step)
        move.start()
        return move

    corner_moves = [
        shift(d_corner_left_ref, corners_high, 0, "tm", -1),
        shift(d_corner_right_ref, corners_low, 1, "tm", 1),
    ]
    exchange = []
    for step in range(1, dp_count):
        s = step - 1
        move = rotation(x_ref.at[step], x_arrived.at[s], x_send.at[s], x_recv.at[s], "dp", step)
        move.start()
        exchange.append(move)
    loads = [
        pltpu.make_async_copy(d_top_ref, to_top, local_sem.at[0]),
        pltpu.make_async_copy(d_bottom_ref, to_bottom, local_sem.at[1]),
        pltpu.make_async_copy(x_ref.at[0], x_held, local_sem.at[2]),
        pltpu.make_async_copy(w_ref, w_held, local_sem.at[3]),
    ]
    for load in loads:
        load.start()
    for move, ref in zip(corner_moves, (corners_high, corners_low)):

        @pl.when(jnp.logical_not(move.has_source))
        def _(ref=ref):
            ref[...] = jnp.zeros_like(ref)

    loads[0].wait()
    loads[1].wait()
    for move in corner_moves:
        move.wait_recv()
    for side, ref in enumerate((to_top, to_bottom)):
        for which in range(2):
            for part, corners in ((slice(0, half), corners_low), (slice(half, 2 * half), corners_high)):
                total = ref[which, part].astype(f32) + corners[which, side].astype(f32)
                ref[which, part] = total.astype(ref.dtype)
    rim_moves = [
        shift(to_top, from_bottom_ref, 2, "height", -1),
        shift(to_bottom, from_top_ref, 3, "height", 1),
        shift(d_left_ref, from_right_ref, 4, "tm", -1),
        shift(d_right_ref, from_left_ref, 5, "tm", 1),
    ]
    loads[2].wait()
    loads[3].wait()
    returned = []
    for step in range(1, dp_count):
        s = step - 1
        exchange[s].wait_recv()
        for tile in tiles_of(w_held.shape[1]):
            y_held[s, :, tile] = contract(x_arrived[s], w_held[:, tile], 0).astype(y_held.dtype)
        move = rotation(
            y_held.at[s], arrived_ref.at[s], y_send.at[s], y_recv.at[s], "dp", -step
        )
        move.start()
        returned.append(move)
    for tile in tiles_of(w_held.shape[1]):
        own_ref[:, tile] = contract(x_held[...], w_held[:, tile], 0)
    for move in rim_moves:
        move.wait_recv()
    for move in corner_moves + rim_moves:
        move.wait_send()
    for move in exchange:
        move.wait_send()
    for move in returned:
        move.wait()


def give(x, w, pieces):
    top, left, corner = pieces[0].shape, pieces[2].shape, pieces[4].shape
    others = lax.axis_size("dp") - 1
    slots = max(others, 1)
    bf16 = jnp.bfloat16
    dma = pltpu.SemaphoreType.DMA
    count, dim = x.shape[1], w.shape[1]
    outs = [jax.ShapeDtypeStruct((count, dim), jnp.float32)]
    outs += [jax.ShapeDtypeStruct(s, bf16) for s in ((slots, count, dim), top, top, left, left)]
    anywhere = pl.BlockSpec(memory_space=pl.ANY)
    return pl.pallas_call(
        give_kernel,
        out_shape=outs,
        in_specs=[anywhere] * 8,
        out_specs=[pl.BlockSpec(memory_space=pltpu.VMEM)] + [anywhere] * 5,
        scratch_shapes=[
            pltpu.VMEM(w.shape, bf16),
            pltpu.VMEM(x.shape[1:], bf16),
            pltpu.VMEM((slots,) + x.shape[1:], bf16),
            pltpu.VMEM((slots, count, dim), bf16),
            pltpu.VMEM(corner, bf16),
            pltpu.VMEM(corner, bf16),
            pltpu.VMEM(top, bf16),
            pltpu.VMEM(top, bf16),
            dma((6,)),
            dma((6,)),
            dma((4,)),
        ]
        + [dma((slots,))] * 4,
        compiler_params=pltpu.CompilerParams(
            collective_id=1, has_side_effects=True, vmem_limit_bytes=48 * 1024 * 1024
        ),
        name="give",
    )(x, w, *pieces)


def body(queries, keys, values, projection, d_outputs):
    f32, bf16 = jnp.float32, jnp.bfloat16
    q, k, v = queries[0], keys[0], values[0]
    frames, rows, cols, dim = q.shape
    tile_len = frames // 2
    query_count = frames * rows * cols
    depth = projection.shape[0]
    dp_count, dp_index = lax.axis_size("dp"), lax.axis_index("dp")

    *pieces, parts = fetch(k, v, d_outputs[0], projection)
    d_attended = jnp.zeros((query_count, dim), bf16)
    for step in range(dp_count):
        owner = lax.rem(dp_index + step, dp_count)
        d_attended = lax.dynamic_update_slice_in_dim(d_attended, parts[step], owner * depth, 1)

    bias = window_bias(tile_len, cols, TWIDE)
    attended, d_queries, d_own, *d_pieces = attention(bias, q, k, v, pieces, d_attended)

    sliced = []
    for step in range(dp_count):
        owner = lax.rem(dp_index + step, dp_count)
        sliced.append(lax.dynamic_slice_in_dim(attended, owner * depth, depth, 1))
    own, arrived, from_top, from_bottom, from_left, from_right = give(
        jnp.stack(sliced), projection, d_pieces
    )

    def present(array, axis, step):
        index = lax.axis_index(axis)
        there = (index - step >= 0) & (index - step < lax.axis_size(axis))
        return jnp.where(there, array.astype(f32), 0.0)

    summed = d_own + jnp.concatenate(
        (present(from_left, "tm", 1), present(from_right, "tm", -1)), axis=1
    )
    summed = summed + jnp.concatenate(
        (present(from_top, "height", 1), present(from_bottom, "height", -1)), axis=2
    )
    summed = summed.astype(bf16)
    outputs = own
    for step in range(1, dp_count):
        outputs = outputs + arrived[step - 1].astype(f32)
    outputs = outputs.astype(bf16)
    return (
        outputs.reshape(d_outputs.shape),
        d_queries[None],
        summed[0][None],
        summed[1][None],
    )


def solution(mesh):
    spread = P("dp", "tm", "height", None, None)
    in_specs = (spread, spread, spread, P("dp", None), spread)
    return jax.shard_map(
        body, mesh=mesh, in_specs=in_specs, out_specs=(spread,) * 4, check_vma=False
    )
```

```python
import functools
import math

import jax
import jax.numpy as jnp
import numpy as np
from jax import lax
from jax.experimental import pallas as pl
from jax.experimental.pallas import tpu as pltpu
from jax.sharding import PartitionSpec as P

HEADS = 20
HDIM = 128
TWIDE = 4
TILES_W = 2

FAR = -1e30
VMEM_LIMIT = 60 * 1024 * 1024


def key_tiles():
    own, low, high = (1, 2), (0,), (3,)
    return (
        (own, own),
        (own, low),
        (own, high),
        (low, own),
        (high, own),
        (low, low),
        (low, high),
        (high, low),
        (high, high),
    )


def tile_coords(tile_len, cols):
    frames, rows = [], []
    for frame_tiles, row_tiles in key_tiles():
        f = np.repeat(np.array(frame_tiles), tile_len)
        r = np.repeat(np.array(row_tiles), tile_len)
        frames.append(np.broadcast_to(f[:, None, None], (len(f), len(r), cols)).reshape(-1))
        rows.append(np.broadcast_to(r[None, :, None], (len(f), len(r), cols)).reshape(-1))
    return np.concatenate(frames), np.concatenate(rows)


def window_bias(tile_len, cols, tile_cols):
    frames, rows = tile_coords(tile_len, cols)
    query_count = 4 * tile_len * tile_len * cols
    query_frames, query_rows = frames[:query_count], rows[:query_count]
    column_tiles = np.arange(cols) // tile_cols
    key_columns = np.tile(column_tiles, len(frames) // cols)
    query_columns = np.tile(column_tiles, query_count // cols)
    inside = np.abs(frames[:, None] - query_frames[None]) <= 1
    inside &= np.abs(rows[:, None] - query_rows[None]) <= 1
    inside &= np.abs(key_columns[:, None] - query_columns[None]) <= 1
    frame_block, frame_blocks = lax.axis_index("tm"), lax.axis_size("tm")
    row_block, row_blocks = lax.axis_index("height"), lax.axis_size("height")
    frame_tile = 2 * frame_block + jnp.asarray(frames, jnp.int32)[:, None] - 1
    row_tile = 2 * row_block + jnp.asarray(rows, jnp.int32)[:, None] - 1
    present = (frame_tile >= 0) & (frame_tile < 2 * frame_blocks)
    present = present & (row_tile >= 0) & (row_tile < 2 * row_blocks)
    return jnp.where(present & jnp.asarray(inside), 0.0, FAR).astype(jnp.float32)


def rows_of(value):
    return value.astype(jnp.float32).reshape(-1, value.shape[-1]).astype(jnp.bfloat16)


def attention_kernel(
    heads,
    scaling,
    bias_ref,
    q_ref,
    k_ref,
    v_ref,
    top_ref,
    bottom_ref,
    left_ref,
    right_ref,
    corner_left_ref,
    corner_right_ref,
    da_ref,
    att_ref,
    dq_ref,
    d_own_ref,
    d_top_ref,
    d_bottom_ref,
    d_left_ref,
    d_right_ref,
    d_corner_left_ref,
    d_corner_right_ref,
):
    f32 = jnp.float32

    def gather(which, own_ref, cols):
        parts = [rows_of(own_ref[:, :, :, cols])]
        for ref in (top_ref, bottom_ref, left_ref, right_ref):
            parts.append(rows_of(ref[which, :, :, :, cols]))
        for ref in (corner_left_ref, corner_right_ref):
            for side in range(2):
                parts.append(rows_of(ref[which, side, :, :, :, cols]))
        return jnp.concatenate(parts, axis=0)

    def scatter(which, grads, cols):
        start = 0
        for ref in (d_own_ref, d_top_ref, d_bottom_ref, d_left_ref, d_right_ref):
            shape = ref.shape[1:-1] + (HDIM,)
            count = shape[0] * shape[1] * shape[2]
            part = grads[start : start + count].reshape(shape)
            ref[which, :, :, :, cols] = part.astype(ref.dtype)
            start += count
        for ref in (d_corner_left_ref, d_corner_right_ref):
            shape = ref.shape[2:-1] + (HDIM,)
            count = shape[0] * shape[1] * shape[2]
            for side in range(2):
                part = grads[start : start + count].reshape(shape)
                ref[which, side, :, :, :, cols] = part.astype(ref.dtype)
                start += count

    for head in range(heads):
        cols = slice(head * HDIM, (head + 1) * HDIM)
        q = rows_of(q_ref[:, :, :, cols])
        k = gather(0, k_ref, cols)
        v = gather(1, v_ref, cols)
        da = da_ref[:, cols]
        scores = lax.dot_general(k, q, (((1,), (1,)), ((), ())), preferred_element_type=f32)
        scores = scores * scaling + bias_ref[...]
        largest = jnp.max(scores, axis=0, keepdims=True)
        weights = jnp.exp(scores - largest)
        inverse = 1.0 / jnp.sum(weights, axis=0, keepdims=True)
        probs = (weights * inverse).astype(jnp.bfloat16)
        att = lax.dot_general(probs, v, (((0,), (0,)), ((), ())), preferred_element_type=f32)
        att_ref[:, cols] = att.astype(att_ref.dtype)
        wide = probs.astype(f32)
        d_probs = lax.dot_general(v, da, (((1,), (1,)), ((), ())), preferred_element_type=f32)
        row_dot = jnp.sum(wide * d_probs, axis=0, keepdims=True)
        d_scores = (wide * (d_probs - row_dot) * scaling).astype(jnp.bfloat16)
        dq = lax.dot_general(d_scores, k, (((0,), (0,)), ((), ())), preferred_element_type=f32)
        shape = dq_ref.shape[:-1] + (HDIM,)
        dq_ref[:, :, :, cols] = dq.reshape(shape).astype(dq_ref.dtype)
        scatter(0, jnp.dot(d_scores, q, preferred_element_type=f32), cols)
        scatter(1, jnp.dot(probs, da, preferred_element_type=f32), cols)


def attention(bias, q, k, v, pieces, da):
    width = 2 * HDIM if HEADS % 2 == 0 else HDIM
    dim = q.shape[-1]

    def blocked(array):
        lead = array.ndim - 1
        return pl.BlockSpec(array.shape[:-1] + (width,), lambda i: (0,) * lead + (i,))

    operands = (q, k, v, *pieces, da)
    grads = [jax.ShapeDtypeStruct((2,) + k.shape, jnp.float32)]
    grads += [jax.ShapeDtypeStruct(p.shape, jnp.bfloat16) for p in pieces]
    outs = [jax.ShapeDtypeStruct(da.shape, jnp.bfloat16), jax.ShapeDtypeStruct(q.shape, q.dtype)]
    outs += grads
    keys, queries = bias.shape
    moved = 2 * sum(math.prod(a.shape) for a in operands + tuple(outs))
    return pl.pallas_call(
        functools.partial(attention_kernel, width // HDIM, 1.0 / math.sqrt(HDIM)),
        grid=(dim // width,),
        out_shape=outs,
        in_specs=[pl.BlockSpec(bias.shape, lambda i: (0, 0))] + [blocked(a) for a in operands],
        out_specs=[blocked(o) for o in outs],
        compiler_params=pltpu.CompilerParams(vmem_limit_bytes=VMEM_LIMIT),
        cost_estimate=pl.CostEstimate(
            flops=12 * keys * queries * dim,
            bytes_accessed=moved,
            transcendentals=keys * queries * dim // HDIM,
        ),
        name="attention",
    )(bias, *operands)


MESH = pl.DeviceIdType.MESH


class Shift:
    def __init__(self, src, dst, send, recv, axis, step):
        count, index = lax.axis_size(axis), lax.axis_index(axis)
        self.has_target = (index + step >= 0) & (index + step < count)
        self.has_source = (index - step >= 0) & (index - step < count)
        target = lax.rem(index + step + count, count)
        self.copy = pltpu.make_async_remote_copy(
            src_ref=src,
            dst_ref=dst,
            send_sem=send,
            recv_sem=recv,
            device_id={axis: target},
            device_id_type=MESH,
        )

    def start(self):
        pl.when(self.has_target)(self.copy.start)

    def wait_recv(self):
        pl.when(self.has_source)(self.copy.wait_recv)

    def wait_send(self):
        pl.when(self.has_target)(self.copy.wait_send)


def rotation(src, dst, send, recv, axis, step):
    count, index = lax.axis_size(axis), lax.axis_index(axis)
    target = lax.rem(index + step + count, count)
    return pltpu.make_async_remote_copy(
        src_ref=src,
        dst_ref=dst,
        send_sem=send,
        recv_sem=recv,
        device_id={axis: target},
        device_id_type=MESH,
    )


def greet():
    barrier = pltpu.get_barrier_semaphore()
    expected = 0
    for axis in ("tm", "height"):
        count, index = lax.axis_size(axis), lax.axis_index(axis)
        for step in (-1, 1):
            there = (index + step >= 0) & (index + step < count)
            target = lax.rem(index + step + count, count)

            @pl.when(there)
            def _(axis=axis, target=target):
                pl.semaphore_signal(
                    barrier, inc=1, device_id={axis: target}, device_id_type=MESH
                )

            expected = expected + jnp.where(there, 1, 0)
    count, index = lax.axis_size("dp"), lax.axis_index("dp")
    for step in range(1, count):
        target = lax.rem(index + step, count)
        pl.semaphore_signal(barrier, inc=1, device_id={"dp": target}, device_id_type=MESH)
    pl.semaphore_wait(barrier, expected + (count - 1))


def tiles_of(width):
    tile = 2 * HDIM if width % (2 * HDIM) == 0 else width
    return [slice(i, i + tile) for i in range(0, width, tile)]


def contract(x, weight, weight_axis):
    return lax.dot_general(
        x, weight, (((1,), (weight_axis,)), ((), ())), preferred_element_type=jnp.float32
    )


def fetch_kernel(
    k_ref,
    v_ref,
    x_ref,
    w_ref,
    top_ref,
    bottom_ref,
    left_ref,
    right_ref,
    corner_left_ref,
    corner_right_ref,
    parts_ref,
    w_held,
    x_held,
    x_arrived,
    part_held,
    send_sem,
    recv_sem,
    local_sem,
    x_send,
    x_recv,
    part_send,
    part_recv,
):
    dp_count = lax.axis_size("dp")
    half = k_ref.shape[0] // 2
    greet()
    first, filled = [], []

    def shift(src, dst, filler, axis, step, into):
        t = len(first) + (0 if into is first else len(into))
        move = Shift(src, dst, send_sem.at[t], recv_sem.at[t], axis, step)
        fill = pltpu.make_async_copy(filler, dst, local_sem.at[t])
        move.start()
        pl.when(jnp.logical_not(move.has_source))(fill.start)
        into.append((move, fill))

    for which, ref in enumerate((k_ref, v_ref)):
        low, high = ref.at[:, :half], ref.at[:, half:]
        shift(high, top_ref.at[which], high, "height", 1, first)
        shift(low, bottom_ref.at[which], low, "height", -1, first)
    exchange = []
    for step in range(1, dp_count):
        s = step - 1
        move = rotation(x_ref, x_arrived.at[s], x_send.at[s], x_recv.at[s], "dp", step)
        move.start()
        exchange.append(move)
    for which, ref in enumerate((k_ref, v_ref)):
        low, high = ref.at[:half], ref.at[half:]
        shift(high, left_ref.at[which], high, "tm", 1, first)
        shift(low, right_ref.at[which], low, "tm", -1, first)
    load_w = pltpu.make_async_copy(w_ref, w_held, local_sem.at[12])
    load_x = pltpu.make_async_copy(x_ref, x_held, local_sem.at[13])
    load_x.start()
    load_w.start()
    load_x.wait()
    load_w.wait()

    def multiply(block, slot):
        x = rows_of(block)
        for tile in tiles_of(w_held.shape[0]):
            part_held[slot, :, tile] = contract(x, w_held[tile, :], 1).astype(part_held.dtype)

    multiply(x_held[...], 0)
    keep = pltpu.make_async_copy(part_held.at[0], parts_ref.at[0], local_sem.at[14])
    keep.start()
    returned = []
    for step in range(1, dp_count):
        s = step - 1
        exchange[s].wait_recv()
        multiply(x_arrived[s], step)
        move = rotation(
            part_held.at[step], parts_ref.at[step], part_send.at[s], part_recv.at[s], "dp", -step
        )
        move.start()
        returned.append(move)

    def settle(move, fill):
        move.wait_recv()
        pl.when(jnp.logical_not(move.has_source))(fill.wait)

    second = []
    for move, fill in first[:4]:
        settle(move, fill)
    for side, ref in enumerate((top_ref, bottom_ref)):
        low, high = ref.at[:, :half], ref.at[:, half:]
        shift(high, corner_left_ref.at[:, side], high, "tm", 1, second)
        shift(low, corner_right_ref.at[:, side], low, "tm", -1, second)
    for move, fill in first[4:] + second:
        settle(move, fill)
    for move, _ in first + second:
        move.wait_send()
    for move in exchange:
        move.wait_send()
    for move in returned:
        move.wait()
    keep.wait()


def fetch(k, v, x, w):
    half = k.shape[0] // 2
    frames, rows, cols, dim = k.shape
    others = lax.axis_size("dp") - 1
    count = frames * rows * cols
    bf16 = jnp.bfloat16
    dma = pltpu.SemaphoreType.DMA
    shapes = [(2, frames, half, cols, dim)] * 2 + [(2, half, rows, cols, dim)] * 2
    shapes += [(2, 2, half, half, cols, dim)] * 2 + [(others + 1, count, w.shape[0])]
    anywhere = pl.BlockSpec(memory_space=pltpu.HBM)
    slots = max(others, 1)
    return pl.pallas_call(
        fetch_kernel,
        out_shape=[jax.ShapeDtypeStruct(s, bf16) for s in shapes],
        in_specs=[anywhere] * 4,
        out_specs=[anywhere] * len(shapes),
        scratch_shapes=[
            pltpu.VMEM(w.shape, bf16),
            pltpu.VMEM(x.shape, bf16),
            pltpu.VMEM((slots,) + x.shape, bf16),
            pltpu.VMEM((others + 1, count, w.shape[0]), bf16),
            dma((12,)),
            dma((12,)),
            dma((15,)),
        ]
        + [dma((slots,))] * 4,
        compiler_params=pltpu.CompilerParams(
            collective_id=0, has_side_effects=True, vmem_limit_bytes=VMEM_LIMIT
        ),
        name="fetch",
    )(k, v, x, w)


def give_kernel(
    x_ref,
    w_ref,
    d_top_ref,
    d_bottom_ref,
    d_left_ref,
    d_right_ref,
    d_corner_left_ref,
    d_corner_right_ref,
    own_ref,
    arrived_ref,
    from_top_ref,
    from_bottom_ref,
    from_left_ref,
    from_right_ref,
    w_held,
    x_held,
    x_arrived,
    y_held,
    corners_low,
    corners_high,
    to_top,
    to_bottom,
    send_sem,
    recv_sem,
    local_sem,
    x_send,
    x_recv,
    y_send,
    y_recv,
):
    dp_count = lax.axis_size("dp")
    half = d_left_ref.shape[1]
    f32 = jnp.float32
    greet()

    def shift(src, dst, t, axis, step):
        move = Shift(src, dst, send_sem.at[t], recv_sem.at[t], axis, step)
        move.start()
        return move

    corner_moves = [
        shift(d_corner_left_ref, corners_high, 0, "tm", -1),
        shift(d_corner_right_ref, corners_low, 1, "tm", 1),
    ]
    exchange = []
    for step in range(1, dp_count):
        s = step - 1
        move = rotation(x_ref.at[step], x_arrived.at[s], x_send.at[s], x_recv.at[s], "dp", step)
        move.start()
        exchange.append(move)
    loads = [
        pltpu.make_async_copy(d_top_ref, to_top, local_sem.at[0]),
        pltpu.make_async_copy(d_bottom_ref, to_bottom, local_sem.at[1]),
        pltpu.make_async_copy(x_ref.at[0], x_held, local_sem.at[2]),
        pltpu.make_async_copy(w_ref, w_held, local_sem.at[3]),
    ]
    for load in loads:
        load.start()
    for move, ref in zip(corner_moves, (corners_high, corners_low)):

        @pl.when(jnp.logical_not(move.has_source))
        def _(ref=ref):
            ref[...] = jnp.zeros_like(ref)

    loads[0].wait()
    loads[1].wait()
    for move in corner_moves:
        move.wait_recv()
    for side, ref in enumerate((to_top, to_bottom)):
        for which in range(2):
            for part, corners in ((slice(0, half), corners_low), (slice(half, 2 * half), corners_high)):
                total = ref[which, part].astype(f32) + corners[which, side].astype(f32)
                ref[which, part] = total.astype(ref.dtype)
    rim_moves = [
        shift(to_top, from_bottom_ref, 2, "height", -1),
        shift(to_bottom, from_top_ref, 3, "height", 1),
        shift(d_left_ref, from_right_ref, 4, "tm", -1),
        shift(d_right_ref, from_left_ref, 5, "tm", 1),
    ]
    loads[2].wait()
    loads[3].wait()
    returned = []
    for step in range(1, dp_count):
        s = step - 1
        exchange[s].wait_recv()
        for tile in tiles_of(w_held.shape[1]):
            y_held[s, :, tile] = contract(x_arrived[s], w_held[:, tile], 0).astype(y_held.dtype)
        move = rotation(
            y_held.at[s], arrived_ref.at[s], y_send.at[s], y_recv.at[s], "dp", -step
        )
        move.start()
        returned.append(move)
    for tile in tiles_of(w_held.shape[1]):
        own_ref[:, tile] = contract(x_held[...], w_held[:, tile], 0)
    for move in rim_moves:
        move.wait_recv()
    for move in corner_moves + rim_moves:
        move.wait_send()
    for move in exchange:
        move.wait_send()
    for move in returned:
        move.wait()


def give(x, w, pieces):
    top, left, corner = pieces[0].shape, pieces[2].shape, pieces[4].shape
    others = lax.axis_size("dp") - 1
    slots = max(others, 1)
    bf16 = jnp.bfloat16
    dma = pltpu.SemaphoreType.DMA
    count, dim = x.shape[1], w.shape[1]
    outs = [jax.ShapeDtypeStruct((count, dim), jnp.float32)]
    outs += [jax.ShapeDtypeStruct(s, bf16) for s in ((slots, count, dim), top, top, left, left)]
    anywhere = pl.BlockSpec(memory_space=pltpu.HBM)
    return pl.pallas_call(
        give_kernel,
        out_shape=outs,
        in_specs=[anywhere] * 8,
        out_specs=[pl.BlockSpec(memory_space=pltpu.VMEM)] + [anywhere] * 5,
        scratch_shapes=[
            pltpu.VMEM(w.shape, bf16),
            pltpu.VMEM(x.shape[1:], bf16),
            pltpu.VMEM((slots,) + x.shape[1:], bf16),
            pltpu.VMEM((slots, count, dim), bf16),
            pltpu.VMEM(corner, bf16),
            pltpu.VMEM(corner, bf16),
            pltpu.VMEM(top, bf16),
            pltpu.VMEM(top, bf16),
            dma((6,)),
            dma((6,)),
            dma((4,)),
        ]
        + [dma((slots,))] * 4,
        compiler_params=pltpu.CompilerParams(
            collective_id=1, has_side_effects=True, vmem_limit_bytes=VMEM_LIMIT
        ),
        name="give",
    )(x, w, *pieces)


def body(queries, keys, values, projection, d_outputs):
    f32, bf16 = jnp.float32, jnp.bfloat16
    q, k, v = queries[0], keys[0], values[0]
    frames, rows, cols, dim = q.shape
    tile_len = frames // 2
    query_count = frames * rows * cols
    depth = projection.shape[0]
    dp_count, dp_index = lax.axis_size("dp"), lax.axis_index("dp")

    *pieces, parts = fetch(k, v, d_outputs[0], projection)
    d_attended = jnp.zeros((query_count, dim), bf16)
    for step in range(dp_count):
        owner = lax.rem(dp_index + step, dp_count)
        d_attended = lax.dynamic_update_slice_in_dim(d_attended, parts[step], owner * depth, 1)

    bias = window_bias(tile_len, cols, TWIDE)
    attended, d_queries, d_own, *d_pieces = attention(bias, q, k, v, pieces, d_attended)

    sliced = []
    for step in range(dp_count):
        owner = lax.rem(dp_index + step, dp_count)
        sliced.append(lax.dynamic_slice_in_dim(attended, owner * depth, depth, 1))
    own, arrived, from_top, from_bottom, from_left, from_right = give(
        jnp.stack(sliced), projection, d_pieces
    )

    def present(array, axis, step):
        index = lax.axis_index(axis)
        there = (index - step >= 0) & (index - step < lax.axis_size(axis))
        return jnp.where(there, array.astype(f32), 0.0)

    summed = d_own + jnp.concatenate(
        (present(from_left, "tm", 1), present(from_right, "tm", -1)), axis=1
    )
    summed = summed + jnp.concatenate(
        (present(from_top, "height", 1), present(from_bottom, "height", -1)), axis=2
    )
    summed = summed.astype(bf16)
    outputs = own
    for step in range(1, dp_count):
        outputs = outputs + arrived[step - 1].astype(f32)
    outputs = outputs.astype(bf16)
    return (
        outputs.reshape(d_outputs.shape),
        d_queries[None],
        summed[0][None],
        summed[1][None],
    )


def solution(mesh):
    spread = P("dp", "tm", "height", None, None)
    in_specs = (spread, spread, spread, P("dp", None), spread)
    return jax.shard_map(
        body, mesh=mesh, in_specs=in_specs, out_specs=(spread,) * 4, check_vma=False
    )
```

```python
import functools
import math

import jax
import jax.numpy as jnp
import numpy as np
from jax import lax
from jax.experimental import pallas as pl
from jax.experimental.pallas import tpu as pltpu
from jax.sharding import PartitionSpec as P

HEADS = 20
HDIM = 128
TWIDE = 4
TILES_W = 2

FAR = -1e30
VMEM_LIMIT = 60 * 1024 * 1024


def key_tiles():
    own, low, high = (1, 2), (0,), (3,)
    return (
        (own, own),
        (own, low),
        (own, high),
        (low, own),
        (high, own),
        (low, low),
        (low, high),
        (high, low),
        (high, high),
    )


def tile_coords(tile_len, cols):
    frames, rows = [], []
    for frame_tiles, row_tiles in key_tiles():
        f = np.repeat(np.array(frame_tiles), tile_len)
        r = np.repeat(np.array(row_tiles), tile_len)
        frames.append(np.broadcast_to(f[:, None, None], (len(f), len(r), cols)).reshape(-1))
        rows.append(np.broadcast_to(r[None, :, None], (len(f), len(r), cols)).reshape(-1))
    return np.concatenate(frames), np.concatenate(rows)


def window_bias(tile_len, cols, tile_cols):
    frames, rows = tile_coords(tile_len, cols)
    query_count = 4 * tile_len * tile_len * cols
    query_frames, query_rows = frames[:query_count], rows[:query_count]
    column_tiles = np.arange(cols) // tile_cols
    key_columns = np.tile(column_tiles, len(frames) // cols)
    query_columns = np.tile(column_tiles, query_count // cols)
    inside = np.abs(frames[:, None] - query_frames[None]) <= 1
    inside &= np.abs(rows[:, None] - query_rows[None]) <= 1
    inside &= np.abs(key_columns[:, None] - query_columns[None]) <= 1
    frame_block, frame_blocks = lax.axis_index("tm"), lax.axis_size("tm")
    row_block, row_blocks = lax.axis_index("height"), lax.axis_size("height")
    frame_tile = 2 * frame_block + jnp.asarray(frames, jnp.int32)[:, None] - 1
    row_tile = 2 * row_block + jnp.asarray(rows, jnp.int32)[:, None] - 1
    present = (frame_tile >= 0) & (frame_tile < 2 * frame_blocks)
    present = present & (row_tile >= 0) & (row_tile < 2 * row_blocks)
    return jnp.where(present & jnp.asarray(inside), 0.0, FAR).astype(jnp.float32)


def rows_of(value):
    return value.astype(jnp.float32).reshape(-1, value.shape[-1]).astype(jnp.bfloat16)


def attention_kernel(
    heads,
    scaling,
    bias_ref,
    q_ref,
    k_ref,
    v_ref,
    top_ref,
    bottom_ref,
    left_ref,
    right_ref,
    corner_left_ref,
    corner_right_ref,
    da_ref,
    att_ref,
    dq_ref,
    d_own_ref,
    d_top_ref,
    d_bottom_ref,
    d_left_ref,
    d_right_ref,
    d_corner_left_ref,
    d_corner_right_ref,
):
    f32 = jnp.float32

    def gather(which, own_ref, cols):
        parts = [rows_of(own_ref[:, :, :, cols])]
        for ref in (top_ref, bottom_ref, left_ref, right_ref):
            parts.append(rows_of(ref[which, :, :, :, cols]))
        for ref in (corner_left_ref, corner_right_ref):
            for side in range(2):
                parts.append(rows_of(ref[which, side, :, :, :, cols]))
        return jnp.concatenate(parts, axis=0)

    def scatter(which, grads, cols):
        start = 0
        for ref in (d_own_ref, d_top_ref, d_bottom_ref, d_left_ref, d_right_ref):
            shape = ref.shape[1:-1] + (HDIM,)
            count = shape[0] * shape[1] * shape[2]
            part = grads[start : start + count].reshape(shape)
            ref[which, :, :, :, cols] = part.astype(ref.dtype)
            start += count
        for ref in (d_corner_left_ref, d_corner_right_ref):
            shape = ref.shape[2:-1] + (HDIM,)
            count = shape[0] * shape[1] * shape[2]
            for side in range(2):
                part = grads[start : start + count].reshape(shape)
                ref[which, side, :, :, :, cols] = part.astype(ref.dtype)
                start += count

    for head in range(heads):
        cols = slice(head * HDIM, (head + 1) * HDIM)
        q = rows_of(q_ref[:, :, :, cols])
        k = gather(0, k_ref, cols)
        v = gather(1, v_ref, cols)
        da = da_ref[:, cols]
        scores = lax.dot_general(k, q, (((1,), (1,)), ((), ())), preferred_element_type=f32)
        scores = scores * scaling + bias_ref[...]
        largest = jnp.max(scores, axis=0, keepdims=True)
        weights = jnp.exp(scores - largest)
        inverse = 1.0 / jnp.sum(weights, axis=0, keepdims=True)
        probs = (weights * inverse).astype(jnp.bfloat16)
        att = lax.dot_general(probs, v, (((0,), (0,)), ((), ())), preferred_element_type=f32)
        att_ref[:, cols] = att.astype(att_ref.dtype)
        wide = probs.astype(f32)
        d_probs = lax.dot_general(v, da, (((1,), (1,)), ((), ())), preferred_element_type=f32)
        row_dot = jnp.sum(wide * d_probs, axis=0, keepdims=True)
        d_scores = (wide * (d_probs - row_dot) * scaling).astype(jnp.bfloat16)
        dq = lax.dot_general(d_scores, k, (((0,), (0,)), ((), ())), preferred_element_type=f32)
        shape = dq_ref.shape[:-1] + (HDIM,)
        dq_ref[:, :, :, cols] = dq.reshape(shape).astype(dq_ref.dtype)
        scatter(0, jnp.dot(d_scores, q, preferred_element_type=f32), cols)
        scatter(1, jnp.dot(probs, da, preferred_element_type=f32), cols)


def attention(bias, q, k, v, pieces, da):
    width = 2 * HDIM if HEADS % 2 == 0 else HDIM
    dim = q.shape[-1]

    def blocked(array):
        lead = array.ndim - 1
        return pl.BlockSpec(array.shape[:-1] + (width,), lambda i: (0,) * lead + (i,))

    operands = (q, k, v, *pieces, da)
    grads = [jax.ShapeDtypeStruct((2,) + k.shape, jnp.float32)]
    grads += [jax.ShapeDtypeStruct(p.shape, jnp.bfloat16) for p in pieces]
    outs = [jax.ShapeDtypeStruct(da.shape, jnp.bfloat16), jax.ShapeDtypeStruct(q.shape, q.dtype)]
    outs += grads
    keys, queries = bias.shape
    moved = 2 * sum(math.prod(a.shape) for a in operands + tuple(outs))
    return pl.pallas_call(
        functools.partial(attention_kernel, width // HDIM, 1.0 / math.sqrt(HDIM)),
        grid=(dim // width,),
        out_shape=outs,
        in_specs=[pl.BlockSpec(bias.shape, lambda i: (0, 0))] + [blocked(a) for a in operands],
        out_specs=[blocked(o) for o in outs],
        compiler_params=pltpu.CompilerParams(vmem_limit_bytes=VMEM_LIMIT),
        cost_estimate=pl.CostEstimate(
            flops=12 * keys * queries * dim,
            bytes_accessed=moved,
            transcendentals=keys * queries * dim // HDIM,
        ),
        name="attention",
    )(bias, *operands)


MESH = pl.DeviceIdType.MESH


class Shift:
    def __init__(self, src, dst, send, recv, axis, step):
        count, index = lax.axis_size(axis), lax.axis_index(axis)
        self.has_target = (index + step >= 0) & (index + step < count)
        self.has_source = (index - step >= 0) & (index - step < count)
        target = lax.rem(index + step + count, count)
        self.copy = pltpu.make_async_remote_copy(
            src_ref=src,
            dst_ref=dst,
            send_sem=send,
            recv_sem=recv,
            device_id={axis: target},
            device_id_type=MESH,
        )

    def start(self):
        pl.when(self.has_target)(self.copy.start)

    def wait_recv(self):
        pl.when(self.has_source)(self.copy.wait_recv)

    def wait_send(self):
        pl.when(self.has_target)(self.copy.wait_send)


def rotation(src, dst, send, recv, axis, step):
    count, index = lax.axis_size(axis), lax.axis_index(axis)
    target = lax.rem(index + step + count, count)
    return pltpu.make_async_remote_copy(
        src_ref=src,
        dst_ref=dst,
        send_sem=send,
        recv_sem=recv,
        device_id={axis: target},
        device_id_type=MESH,
    )


def greet():
    barrier = pltpu.get_barrier_semaphore()
    expected = 0
    for axis in ("tm", "height"):
        count, index = lax.axis_size(axis), lax.axis_index(axis)
        for step in (-1, 1):
            there = (index + step >= 0) & (index + step < count)
            target = lax.rem(index + step + count, count)

            @pl.when(there)
            def _(axis=axis, target=target):
                pl.semaphore_signal(
                    barrier, inc=1, device_id={axis: target}, device_id_type=MESH
                )

            expected = expected + jnp.where(there, 1, 0)
    count, index = lax.axis_size("dp"), lax.axis_index("dp")
    for step in range(1, count):
        target = lax.rem(index + step, count)
        pl.semaphore_signal(barrier, inc=1, device_id={"dp": target}, device_id_type=MESH)
    pl.semaphore_wait(barrier, expected + (count - 1))


def tiles_of(width):
    tile = 2 * HDIM if width % (2 * HDIM) == 0 else width
    return [slice(i, i + tile) for i in range(0, width, tile)]


def contract(x, weight, weight_axis):
    return lax.dot_general(
        x, weight, (((1,), (weight_axis,)), ((), ())), preferred_element_type=jnp.float32
    )


def fetch_kernel(
    k_ref,
    v_ref,
    x_ref,
    w_ref,
    top_ref,
    bottom_ref,
    left_ref,
    right_ref,
    corner_left_ref,
    corner_right_ref,
    parts_ref,
    w_held,
    x_held,
    x_arrived,
    part_held,
    send_sem,
    recv_sem,
    local_sem,
    x_send,
    x_recv,
    part_send,
    part_recv,
):
    dp_count = lax.axis_size("dp")
    half = k_ref.shape[0] // 2
    greet()
    first, filled = [], []

    def shift(src, dst, filler, axis, step, into):
        t = len(first) + (0 if into is first else len(into))
        move = Shift(src, dst, send_sem.at[t], recv_sem.at[t], axis, step)
        fill = pltpu.make_async_copy(filler, dst, local_sem.at[t])
        move.start()
        pl.when(jnp.logical_not(move.has_source))(fill.start)
        into.append((move, fill))

    for which, ref in enumerate((k_ref, v_ref)):
        low, high = ref.at[:, :half], ref.at[:, half:]
        shift(high, top_ref.at[which], high, "height", 1, first)
        shift(low, bottom_ref.at[which], low, "height", -1, first)
    exchange = []
    for step in range(1, dp_count):
        s = step - 1
        move = rotation(x_ref, x_arrived.at[s], x_send.at[s], x_recv.at[s], "dp", step)
        move.start()
        exchange.append(move)
    for which, ref in enumerate((k_ref, v_ref)):
        low, high = ref.at[:half], ref.at[half:]
        shift(high, left_ref.at[which], high, "tm", 1, first)
        shift(low, right_ref.at[which], low, "tm", -1, first)
    load_w = pltpu.make_async_copy(w_ref, w_held, local_sem.at[12])
    load_x = pltpu.make_async_copy(x_ref, x_held, local_sem.at[13])
    load_x.start()
    load_w.start()
    load_x.wait()
    load_w.wait()

    def multiply(block, slot):
        x = rows_of(block)
        for tile in tiles_of(w_held.shape[0]):
            part_held[slot, :, tile] = contract(x, w_held[tile, :], 1).astype(part_held.dtype)

    multiply(x_held[...], 0)
    keep = pltpu.make_async_copy(part_held.at[0], parts_ref.at[0], local_sem.at[14])
    keep.start()
    returned = []
    for step in range(1, dp_count):
        s = step - 1
        exchange[s].wait_recv()
        multiply(x_arrived[s], step)
        move = rotation(
            part_held.at[step], parts_ref.at[step], part_send.at[s], part_recv.at[s], "dp", -step
        )
        move.start()
        returned.append(move)

    def settle(move, fill):
        move.wait_recv()
        pl.when(jnp.logical_not(move.has_source))(fill.wait)

    second = []
    for move, fill in first[:4]:
        settle(move, fill)
    for side, ref in enumerate((top_ref, bottom_ref)):
        low, high = ref.at[:, :half], ref.at[:, half:]
        shift(high, corner_left_ref.at[:, side], high, "tm", 1, second)
        shift(low, corner_right_ref.at[:, side], low, "tm", -1, second)
    for move, fill in first[4:] + second:
        settle(move, fill)
    for move, _ in first + second:
        move.wait_send()
    for move in exchange:
        move.wait_send()
    for move in returned:
        move.wait()
    keep.wait()


def fetch(k, v, x, w):
    half = k.shape[0] // 2
    frames, rows, cols, dim = k.shape
    others = lax.axis_size("dp") - 1
    count = frames * rows * cols
    bf16 = jnp.bfloat16
    dma = pltpu.SemaphoreType.DMA
    shapes = [(2, frames, half, cols, dim)] * 2 + [(2, half, rows, cols, dim)] * 2
    shapes += [(2, 2, half, half, cols, dim)] * 2 + [(others + 1, count, w.shape[0])]
    anywhere = pl.BlockSpec(memory_space=pltpu.HBM)
    slots = max(others, 1)
    return pl.pallas_call(
        fetch_kernel,
        out_shape=[jax.ShapeDtypeStruct(s, bf16) for s in shapes],
        in_specs=[anywhere] * 4,
        out_specs=[anywhere] * len(shapes),
        scratch_shapes=[
            pltpu.VMEM(w.shape, bf16),
            pltpu.VMEM(x.shape, bf16),
            pltpu.VMEM((slots,) + x.shape, bf16),
            pltpu.VMEM((others + 1, count, w.shape[0]), bf16),
            dma((12,)),
            dma((12,)),
            dma((15,)),
        ]
        + [dma((slots,))] * 4,
        compiler_params=pltpu.CompilerParams(
            collective_id=0, has_side_effects=True, vmem_limit_bytes=VMEM_LIMIT
        ),
        name="fetch",
    )(k, v, x, w)


def give_kernel(
    w_ref,
    d_own_ref,
    x_ref,
    to_top_ref,
    to_bottom_ref,
    d_left_ref,
    d_right_ref,
    d_corner_left_ref,
    d_corner_right_ref,
    outputs_ref,
    dk_ref,
    dv_ref,
    own_ref,
    total_ref,
    arrived_ref,
    from_top_ref,
    from_bottom_ref,
    from_left_ref,
    from_right_ref,
    w_held,
    x_arrived,
    y_held,
    corners_low,
    corners_high,
    to_top,
    to_bottom,
    send_sem,
    recv_sem,
    local_sem,
    x_send,
    x_recv,
    y_send,
    y_recv,
):
    dp_count = lax.axis_size("dp")
    half = d_left_ref.shape[1]
    f32 = jnp.float32
    greet()

    def shift(src, dst, t, axis, step):
        move = Shift(src, dst, send_sem.at[t], recv_sem.at[t], axis, step)
        move.start()
        return move

    corner_moves = [
        shift(d_corner_left_ref, corners_high, 0, "tm", -1),
        shift(d_corner_right_ref, corners_low, 1, "tm", 1),
    ]
    exchange = []
    for step in range(1, dp_count):
        s = step - 1
        move = rotation(x_ref.at[step], x_arrived.at[s], x_send.at[s], x_recv.at[s], "dp", step)
        move.start()
        exchange.append(move)
    loads = [
        pltpu.make_async_copy(w_ref, w_held, local_sem.at[0]),
        pltpu.make_async_copy(d_own_ref, total_ref, local_sem.at[1]),
    ]
    for load in loads:
        load.start()
    for move, ref in zip(corner_moves, (corners_high, corners_low)):

        @pl.when(jnp.logical_not(move.has_source))
        def _(ref=ref):
            ref[...] = jnp.zeros_like(ref)

    for move in corner_moves:
        move.wait_recv()
    for side, (ref, sent) in enumerate(((to_top_ref, to_top), (to_bottom_ref, to_bottom))):
        for which in range(2):
            for part, corners in ((slice(0, half), corners_low), (slice(half, 2 * half), corners_high)):
                total = ref[which, part].astype(f32) + corners[which, side].astype(f32)
                sent[which, part] = total.astype(sent.dtype)
    rim_moves = [
        shift(to_top, from_bottom_ref, 2, "height", -1),
        shift(to_bottom, from_top_ref, 3, "height", 1),
        shift(d_left_ref, from_right_ref, 4, "tm", -1),
        shift(d_right_ref, from_left_ref, 5, "tm", 1),
    ]
    rim_refs = (from_bottom_ref, from_top_ref, from_right_ref, from_left_ref)
    for move, ref in zip(rim_moves, rim_refs):

        @pl.when(jnp.logical_not(move.has_source))
        def _(ref=ref):
            ref[...] = jnp.zeros_like(ref)

    loads[0].wait()
    returned = []
    for step in range(1, dp_count):
        s = step - 1
        exchange[s].wait_recv()
        for tile in tiles_of(w_held.shape[1]):
            y_held[s, :, tile] = contract(x_arrived[s], w_held[:, tile], 0).astype(y_held.dtype)
        move = rotation(
            y_held.at[s], arrived_ref.at[s], y_send.at[s], y_recv.at[s], "dp", -step
        )
        move.start()
        returned.append(move)
    for tile in tiles_of(w_held.shape[1]):
        own_ref[:, tile] = contract(x_ref[0], w_held[:, tile], 0)
    loads[1].wait()
    for move in rim_moves:
        move.wait_recv()
    halves = (slice(0, half), slice(half, 2 * half))
    for which, ref in enumerate((dk_ref, dv_ref)):
        for f, from_frames in zip(halves, (from_left_ref, from_right_ref)):
            for r, from_rows in zip(halves, (from_top_ref, from_bottom_ref)):
                total = total_ref[which, f, r] + from_frames[which, :, r].astype(f32)
                total = total + from_rows[which, f].astype(f32)
                ref[f, r] = total.astype(ref.dtype)
    for move in returned:
        move.wait_recv()
    for tile in tiles_of(w_held.shape[1]):
        total = own_ref[:, tile]
        for s in range(dp_count - 1):
            total = total + arrived_ref[s, :, tile].astype(f32)
        shape = outputs_ref.shape[:-1] + total.shape[-1:]
        outputs_ref[:, :, :, tile] = total.reshape(shape).astype(outputs_ref.dtype)
    for move in corner_moves + rim_moves + exchange + returned:
        move.wait_send()


def give(x, w, d_own, pieces):
    top, left, corner = pieces[0].shape, pieces[2].shape, pieces[4].shape
    others = lax.axis_size("dp") - 1
    slots = max(others, 1)
    bf16 = jnp.bfloat16
    dma = pltpu.SemaphoreType.DMA
    count, dim = x.shape[1], w.shape[1]
    grid = d_own.shape[1:-1]
    outs = [jax.ShapeDtypeStruct(grid + (dim,), bf16)]
    outs += [jax.ShapeDtypeStruct(d_own.shape[1:], bf16)] * 2
    anywhere = pl.BlockSpec(memory_space=pltpu.HBM)
    inside = pl.BlockSpec(memory_space=pltpu.VMEM)
    return pl.pallas_call(
        give_kernel,
        out_shape=outs,
        in_specs=[anywhere] * 2 + [inside] * 7,
        out_specs=[inside] * 3,
        scratch_shapes=[
            pltpu.VMEM((count, dim), jnp.float32),
            pltpu.VMEM(d_own.shape, jnp.float32),
            pltpu.VMEM((slots, count, dim), bf16),
            pltpu.VMEM(top, bf16),
            pltpu.VMEM(top, bf16),
            pltpu.VMEM(left, bf16),
            pltpu.VMEM(left, bf16),
            pltpu.VMEM(w.shape, bf16),
            pltpu.VMEM((slots,) + x.shape[1:], bf16),
            pltpu.VMEM((slots, count, dim), bf16),
            pltpu.VMEM(corner, bf16),
            pltpu.VMEM(corner, bf16),
            pltpu.VMEM(top, bf16),
            pltpu.VMEM(top, bf16),
            dma((6,)),
            dma((6,)),
            dma((2,)),
        ]
        + [dma((slots,))] * 4,
        compiler_params=pltpu.CompilerParams(
            collective_id=1, has_side_effects=True, vmem_limit_bytes=VMEM_LIMIT
        ),
        name="give",
    )(w, d_own, x, *pieces)


def body(queries, keys, values, projection, d_outputs):
    f32, bf16 = jnp.float32, jnp.bfloat16
    q, k, v = queries[0], keys[0], values[0]
    frames, rows, cols, dim = q.shape
    tile_len = frames // 2
    query_count = frames * rows * cols
    depth = projection.shape[0]
    dp_count, dp_index = lax.axis_size("dp"), lax.axis_index("dp")

    *pieces, parts = fetch(k, v, d_outputs[0], projection)
    d_attended = jnp.zeros((query_count, dim), bf16)
    for step in range(dp_count):
        owner = lax.rem(dp_index + step, dp_count)
        d_attended = lax.dynamic_update_slice_in_dim(d_attended, parts[step], owner * depth, 1)

    bias = window_bias(tile_len, cols, TWIDE)
    attended, d_queries, d_own, *d_pieces = attention(bias, q, k, v, pieces, d_attended)

    sliced = []
    for step in range(dp_count):
        owner = lax.rem(dp_index + step, dp_count)
        sliced.append(lax.dynamic_slice_in_dim(attended, owner * depth, depth, 1))
    outputs, d_keys, d_values = give(jnp.stack(sliced), projection, d_own, d_pieces)
    return (outputs[None], d_queries[None], d_keys[None], d_values[None])


def solution(mesh):
    spread = P("dp", "tm", "height", None, None)
    in_specs = (spread, spread, spread, P("dp", None), spread)
    return jax.shard_map(
        body, mesh=mesh, in_specs=in_specs, out_specs=(spread,) * 4, check_vma=False
    )
```

```python
import functools
import math

import jax
import jax.numpy as jnp
import numpy as np
from jax import lax
from jax.experimental import pallas as pl
from jax.experimental.pallas import tpu as pltpu
from jax.sharding import PartitionSpec as P

HEADS = 20
HDIM = 128
TWIDE = 4
TILES_W = 2

FAR = -1e30
VMEM_LIMIT = 60 * 1024 * 1024


def key_tiles():
    own, low, high = (1, 2), (0,), (3,)
    return (
        (own, own),
        (own, low),
        (own, high),
        (low, own),
        (high, own),
        (low, low),
        (low, high),
        (high, low),
        (high, high),
    )


def tile_coords(tile_len, cols):
    frames, rows = [], []
    for frame_tiles, row_tiles in key_tiles():
        f = np.repeat(np.array(frame_tiles), tile_len)
        r = np.repeat(np.array(row_tiles), tile_len)
        frames.append(np.broadcast_to(f[:, None, None], (len(f), len(r), cols)).reshape(-1))
        rows.append(np.broadcast_to(r[None, :, None], (len(f), len(r), cols)).reshape(-1))
    return np.concatenate(frames), np.concatenate(rows)


def window_bias(tile_len, cols, tile_cols):
    frames, rows = tile_coords(tile_len, cols)
    query_count = 4 * tile_len * tile_len * cols
    query_frames, query_rows = frames[:query_count], rows[:query_count]
    column_tiles = np.arange(cols) // tile_cols
    key_columns = np.tile(column_tiles, len(frames) // cols)
    query_columns = np.tile(column_tiles, query_count // cols)
    inside = np.abs(frames[:, None] - query_frames[None]) <= 1
    inside &= np.abs(rows[:, None] - query_rows[None]) <= 1
    inside &= np.abs(key_columns[:, None] - query_columns[None]) <= 1
    frame_block, frame_blocks = lax.axis_index("tm"), lax.axis_size("tm")
    row_block, row_blocks = lax.axis_index("height"), lax.axis_size("height")
    frame_tile = 2 * frame_block + jnp.asarray(frames, jnp.int32)[:, None] - 1
    row_tile = 2 * row_block + jnp.asarray(rows, jnp.int32)[:, None] - 1
    present = (frame_tile >= 0) & (frame_tile < 2 * frame_blocks)
    present = present & (row_tile >= 0) & (row_tile < 2 * row_blocks)
    return jnp.where(present & jnp.asarray(inside), 0.0, FAR).astype(jnp.float32)


def rows_of(value):
    return value.astype(jnp.float32).reshape(-1, value.shape[-1]).astype(jnp.bfloat16)


def attention_kernel(
    heads,
    scaling,
    bias_ref,
    q_ref,
    k_ref,
    v_ref,
    top_ref,
    bottom_ref,
    left_ref,
    right_ref,
    corner_left_ref,
    corner_right_ref,
    da_ref,
    att_ref,
    dq_ref,
    d_own_ref,
    d_top_ref,
    d_bottom_ref,
    d_left_ref,
    d_right_ref,
    d_corner_left_ref,
    d_corner_right_ref,
):
    f32 = jnp.float32

    def gather(which, own_ref, cols):
        parts = [rows_of(own_ref[:, :, :, cols])]
        for ref in (top_ref, bottom_ref, left_ref, right_ref):
            parts.append(rows_of(ref[which, :, :, :, cols]))
        for ref in (corner_left_ref, corner_right_ref):
            for side in range(2):
                parts.append(rows_of(ref[which, side, :, :, :, cols]))
        return jnp.concatenate(parts, axis=0)

    def scatter(which, grads, cols):
        start = 0
        for ref in (d_own_ref, d_top_ref, d_bottom_ref, d_left_ref, d_right_ref):
            shape = ref.shape[1:-1] + (HDIM,)
            count = shape[0] * shape[1] * shape[2]
            part = grads[start : start + count].reshape(shape)
            ref[which, :, :, :, cols] = part.astype(ref.dtype)
            start += count
        for ref in (d_corner_left_ref, d_corner_right_ref):
            shape = ref.shape[2:-1] + (HDIM,)
            count = shape[0] * shape[1] * shape[2]
            for side in range(2):
                part = grads[start : start + count].reshape(shape)
                ref[which, side, :, :, :, cols] = part.astype(ref.dtype)
                start += count

    for head in range(heads):
        cols = slice(head * HDIM, (head + 1) * HDIM)
        q = rows_of(q_ref[:, :, :, cols])
        k = gather(0, k_ref, cols)
        v = gather(1, v_ref, cols)
        da = da_ref[:, cols]
        scores = lax.dot_general(k, q, (((1,), (1,)), ((), ())), preferred_element_type=f32)
        scores = scores * scaling + bias_ref[...]
        largest = jnp.max(scores, axis=0, keepdims=True)
        weights = jnp.exp(scores - largest)
        inverse = 1.0 / jnp.sum(weights, axis=0, keepdims=True)
        probs = (weights * inverse).astype(jnp.bfloat16)
        att = lax.dot_general(probs, v, (((0,), (0,)), ((), ())), preferred_element_type=f32)
        att_ref[:, cols] = att.astype(att_ref.dtype)
        wide = probs.astype(f32)
        d_probs = lax.dot_general(v, da, (((1,), (1,)), ((), ())), preferred_element_type=f32)
        row_dot = jnp.sum(wide * d_probs, axis=0, keepdims=True)
        d_scores = (wide * (d_probs - row_dot) * scaling).astype(jnp.bfloat16)
        dq = lax.dot_general(d_scores, k, (((0,), (0,)), ((), ())), preferred_element_type=f32)
        shape = dq_ref.shape[:-1] + (HDIM,)
        dq_ref[:, :, :, cols] = dq.reshape(shape).astype(dq_ref.dtype)
        scatter(0, jnp.dot(d_scores, q, preferred_element_type=f32), cols)
        scatter(1, jnp.dot(probs, da, preferred_element_type=f32), cols)


def attention(bias, q, k, v, pieces, da):
    width = 2 * HDIM if HEADS % 2 == 0 else HDIM
    dim = q.shape[-1]

    def blocked(array):
        lead = array.ndim - 1
        return pl.BlockSpec(array.shape[:-1] + (width,), lambda i: (0,) * lead + (i,))

    operands = (q, k, v, *pieces, da)
    grads = [jax.ShapeDtypeStruct((2,) + k.shape, jnp.float32)]
    grads += [jax.ShapeDtypeStruct(p.shape, jnp.bfloat16) for p in pieces]
    outs = [jax.ShapeDtypeStruct(da.shape, jnp.bfloat16), jax.ShapeDtypeStruct(q.shape, q.dtype)]
    outs += grads
    keys, queries = bias.shape
    moved = 2 * sum(math.prod(a.shape) for a in operands + tuple(outs))
    return pl.pallas_call(
        functools.partial(attention_kernel, width // HDIM, 1.0 / math.sqrt(HDIM)),
        grid=(dim // width,),
        out_shape=outs,
        in_specs=[pl.BlockSpec(bias.shape, lambda i: (0, 0))] + [blocked(a) for a in operands],
        out_specs=[blocked(o) for o in outs],
        compiler_params=pltpu.CompilerParams(vmem_limit_bytes=VMEM_LIMIT),
        cost_estimate=pl.CostEstimate(
            flops=12 * keys * queries * dim,
            bytes_accessed=moved,
            transcendentals=keys * queries * dim // HDIM,
        ),
        name="attention",
    )(bias, *operands)


MESH = pl.DeviceIdType.MESH


class Shift:
    def __init__(self, src, dst, send, recv, axis, step):
        count, index = lax.axis_size(axis), lax.axis_index(axis)
        self.has_target = (index + step >= 0) & (index + step < count)
        self.has_source = (index - step >= 0) & (index - step < count)
        target = lax.rem(index + step + count, count)
        self.copy = pltpu.make_async_remote_copy(
            src_ref=src,
            dst_ref=dst,
            send_sem=send,
            recv_sem=recv,
            device_id={axis: target},
            device_id_type=MESH,
        )

    def start(self):
        pl.when(self.has_target)(self.copy.start)

    def wait_recv(self):
        pl.when(self.has_source)(self.copy.wait_recv)

    def wait_send(self):
        pl.when(self.has_target)(self.copy.wait_send)


def rotation(src, dst, send, recv, axis, step):
    count, index = lax.axis_size(axis), lax.axis_index(axis)
    target = lax.rem(index + step + count, count)
    return pltpu.make_async_remote_copy(
        src_ref=src,
        dst_ref=dst,
        send_sem=send,
        recv_sem=recv,
        device_id={axis: target},
        device_id_type=MESH,
    )


def greet():
    barrier = pltpu.get_barrier_semaphore()
    expected = 0
    for axis in ("tm", "height"):
        count, index = lax.axis_size(axis), lax.axis_index(axis)
        for step in (-1, 1):
            there = (index + step >= 0) & (index + step < count)
            target = lax.rem(index + step + count, count)

            @pl.when(there)
            def _(axis=axis, target=target):
                pl.semaphore_signal(
                    barrier, inc=1, device_id={axis: target}, device_id_type=MESH
                )

            expected = expected + jnp.where(there, 1, 0)
    count, index = lax.axis_size("dp"), lax.axis_index("dp")
    for step in range(1, count):
        target = lax.rem(index + step, count)
        pl.semaphore_signal(barrier, inc=1, device_id={"dp": target}, device_id_type=MESH)
    pl.semaphore_wait(barrier, expected + (count - 1))


def tiles_of(width):
    tile = 2 * HDIM if width % (2 * HDIM) == 0 else width
    return [slice(i, i + tile) for i in range(0, width, tile)]


def contract(x, weight, weight_axis):
    return lax.dot_general(
        x, weight, (((1,), (weight_axis,)), ((), ())), preferred_element_type=jnp.float32
    )


def fetch_kernel(
    k_ref,
    v_ref,
    x_ref,
    w_ref,
    top_ref,
    bottom_ref,
    left_ref,
    right_ref,
    corner_left_ref,
    corner_right_ref,
    parts_ref,
    w_held,
    x_held,
    x_arrived,
    part_held,
    zeros,
    corner_zeros,
    send_sem,
    recv_sem,
    local_sem,
    x_send,
    x_recv,
    part_send,
    part_recv,
):
    dp_count = lax.axis_size("dp")
    half = k_ref.shape[0] // 2
    zeros[...] = jnp.zeros_like(zeros)
    corner_zeros[...] = jnp.zeros_like(corner_zeros)
    no_rows, no_frames = zeros.at[:, :half], zeros.at[:half]
    greet()
    first, filled = [], []

    def shift(src, dst, filler, axis, step, into):
        t = len(first) + (0 if into is first else len(into))
        move = Shift(src, dst, send_sem.at[t], recv_sem.at[t], axis, step)
        fill = pltpu.make_async_copy(filler, dst, local_sem.at[t])
        move.start()
        pl.when(jnp.logical_not(move.has_source))(fill.start)
        into.append((move, fill))

    for which, ref in enumerate((k_ref, v_ref)):
        low, high = ref.at[:, :half], ref.at[:, half:]
        shift(high, top_ref.at[which], no_rows, "height", 1, first)
        shift(low, bottom_ref.at[which], no_rows, "height", -1, first)
    exchange = []
    for step in range(1, dp_count):
        s = step - 1
        move = rotation(x_ref, x_arrived.at[s], x_send.at[s], x_recv.at[s], "dp", step)
        move.start()
        exchange.append(move)
    for which, ref in enumerate((k_ref, v_ref)):
        low, high = ref.at[:half], ref.at[half:]
        shift(high, left_ref.at[which], no_frames, "tm", 1, first)
        shift(low, right_ref.at[which], no_frames, "tm", -1, first)
    load_w = pltpu.make_async_copy(w_ref, w_held, local_sem.at[12])
    load_x = pltpu.make_async_copy(x_ref, x_held, local_sem.at[13])
    load_x.start()
    load_w.start()
    load_x.wait()
    load_w.wait()

    def multiply(block, slot):
        x = rows_of(block)
        for tile in tiles_of(w_held.shape[0]):
            part_held[slot, :, tile] = contract(x, w_held[tile, :], 1).astype(part_held.dtype)

    multiply(x_held[...], 0)
    keep = pltpu.make_async_copy(part_held.at[0], parts_ref.at[0], local_sem.at[14])
    keep.start()
    returned = []
    for step in range(1, dp_count):
        s = step - 1
        exchange[s].wait_recv()
        multiply(x_arrived[s], step)
        move = rotation(
            part_held.at[step], parts_ref.at[step], part_send.at[s], part_recv.at[s], "dp", -step
        )
        move.start()
        returned.append(move)

    def settle(move, fill):
        move.wait_recv()
        pl.when(jnp.logical_not(move.has_source))(fill.wait)

    second = []
    for move, fill in first[:4]:
        settle(move, fill)
    for side, ref in enumerate((top_ref, bottom_ref)):
        low, high = ref.at[:, :half], ref.at[:, half:]
        shift(high, corner_left_ref.at[:, side], corner_zeros, "tm", 1, second)
        shift(low, corner_right_ref.at[:, side], corner_zeros, "tm", -1, second)
    for move, fill in first[4:] + second:
        settle(move, fill)
    for move, _ in first + second:
        move.wait_send()
    for move in exchange:
        move.wait_send()
    for move in returned:
        move.wait()
    keep.wait()


def fetch(k, v, x, w):
    half = k.shape[0] // 2
    frames, rows, cols, dim = k.shape
    others = lax.axis_size("dp") - 1
    count = frames * rows * cols
    bf16 = jnp.bfloat16
    dma = pltpu.SemaphoreType.DMA
    shapes = [(2, frames, half, cols, dim)] * 2 + [(2, half, rows, cols, dim)] * 2
    shapes += [(2, 2, half, half, cols, dim)] * 2 + [(others + 1, count, w.shape[0])]
    anywhere = pl.BlockSpec(memory_space=pltpu.HBM)
    slots = max(others, 1)
    return pl.pallas_call(
        fetch_kernel,
        out_shape=[jax.ShapeDtypeStruct(s, bf16) for s in shapes],
        in_specs=[anywhere] * 4,
        out_specs=[anywhere] * len(shapes),
        scratch_shapes=[
            pltpu.VMEM(w.shape, bf16),
            pltpu.VMEM(x.shape, bf16),
            pltpu.VMEM((slots,) + x.shape, bf16),
            pltpu.VMEM((others + 1, count, w.shape[0]), bf16),
            pltpu.VMEM(k.shape, bf16),
            pltpu.VMEM((2, half, half, cols, dim), bf16),
            dma((12,)),
            dma((12,)),
            dma((15,)),
        ]
        + [dma((slots,))] * 4,
        compiler_params=pltpu.CompilerParams(
            collective_id=0, has_side_effects=True, vmem_limit_bytes=VMEM_LIMIT
        ),
        name="fetch",
    )(k, v, x, w)


def give_kernel(
    w_ref,
    d_own_ref,
    x_ref,
    to_top_ref,
    to_bottom_ref,
    d_left_ref,
    d_right_ref,
    d_corner_left_ref,
    d_corner_right_ref,
    outputs_ref,
    dk_ref,
    dv_ref,
    own_ref,
    total_ref,
    arrived_ref,
    from_top_ref,
    from_bottom_ref,
    from_left_ref,
    from_right_ref,
    w_held,
    x_arrived,
    y_held,
    corners_low,
    corners_high,
    to_top,
    to_bottom,
    send_sem,
    recv_sem,
    local_sem,
    x_send,
    x_recv,
    y_send,
    y_recv,
):
    dp_count = lax.axis_size("dp")
    half = d_left_ref.shape[1]
    f32 = jnp.float32
    greet()

    def shift(src, dst, t, axis, step):
        move = Shift(src, dst, send_sem.at[t], recv_sem.at[t], axis, step)
        move.start()
        return move

    corner_moves = [
        shift(d_corner_left_ref, corners_high, 0, "tm", -1),
        shift(d_corner_right_ref, corners_low, 1, "tm", 1),
    ]
    exchange = []
    for step in range(1, dp_count):
        s = step - 1
        move = rotation(x_ref.at[step], x_arrived.at[s], x_send.at[s], x_recv.at[s], "dp", step)
        move.start()
        exchange.append(move)
    loads = [
        pltpu.make_async_copy(w_ref, w_held, local_sem.at[0]),
        pltpu.make_async_copy(d_own_ref, total_ref, local_sem.at[1]),
    ]
    for load in loads:
        load.start()
    for move, ref in zip(corner_moves, (corners_high, corners_low)):

        @pl.when(jnp.logical_not(move.has_source))
        def _(ref=ref):
            ref[...] = jnp.zeros_like(ref)

    for move in corner_moves:
        move.wait_recv()
    for side, (ref, sent) in enumerate(((to_top_ref, to_top), (to_bottom_ref, to_bottom))):
        for which in range(2):
            for part, corners in ((slice(0, half), corners_low), (slice(half, 2 * half), corners_high)):
                total = ref[which, part].astype(f32) + corners[which, side].astype(f32)
                sent[which, part] = total.astype(sent.dtype)
    rim_moves = [
        shift(to_top, from_bottom_ref, 2, "height", -1),
        shift(to_bottom, from_top_ref, 3, "height", 1),
        shift(d_left_ref, from_right_ref, 4, "tm", -1),
        shift(d_right_ref, from_left_ref, 5, "tm", 1),
    ]
    rim_refs = (from_bottom_ref, from_top_ref, from_right_ref, from_left_ref)
    for move, ref in zip(rim_moves, rim_refs):

        @pl.when(jnp.logical_not(move.has_source))
        def _(ref=ref):
            ref[...] = jnp.zeros_like(ref)

    loads[0].wait()
    returned = []
    for step in range(1, dp_count):
        s = step - 1
        exchange[s].wait_recv()
        for tile in tiles_of(w_held.shape[1]):
            y_held[s, :, tile] = contract(x_arrived[s], w_held[:, tile], 0).astype(y_held.dtype)
        move = rotation(
            y_held.at[s], arrived_ref.at[s], y_send.at[s], y_recv.at[s], "dp", -step
        )
        move.start()
        returned.append(move)
    for tile in tiles_of(w_held.shape[1]):
        own_ref[:, tile] = contract(x_ref[0], w_held[:, tile], 0)
    loads[1].wait()
    for move in rim_moves:
        move.wait_recv()
    halves = (slice(0, half), slice(half, 2 * half))
    for which, ref in enumerate((dk_ref, dv_ref)):
        for f, from_frames in zip(halves, (from_left_ref, from_right_ref)):
            for r, from_rows in zip(halves, (from_top_ref, from_bottom_ref)):
                total = total_ref[which, f, r] + from_frames[which, :, r].astype(f32)
                total = total + from_rows[which, f].astype(f32)
                ref[f, r] = total.astype(ref.dtype)
    for move in returned:
        move.wait_recv()
    for tile in tiles_of(w_held.shape[1]):
        total = own_ref[:, tile]
        for s in range(dp_count - 1):
            total = total + arrived_ref[s, :, tile].astype(f32)
        shape = outputs_ref.shape[:-1] + total.shape[-1:]
        outputs_ref[:, :, :, tile] = total.reshape(shape).astype(outputs_ref.dtype)
    for move in corner_moves + rim_moves + exchange + returned:
        move.wait_send()


def give(x, w, d_own, pieces):
    top, left, corner = pieces[0].shape, pieces[2].shape, pieces[4].shape
    others = lax.axis_size("dp") - 1
    slots = max(others, 1)
    bf16 = jnp.bfloat16
    dma = pltpu.SemaphoreType.DMA
    count, dim = x.shape[1], w.shape[1]
    grid = d_own.shape[1:-1]
    outs = [jax.ShapeDtypeStruct(grid + (dim,), bf16)]
    outs += [jax.ShapeDtypeStruct(d_own.shape[1:], bf16)] * 2
    anywhere = pl.BlockSpec(memory_space=pltpu.HBM)
    inside = pl.BlockSpec(memory_space=pltpu.VMEM)
    return pl.pallas_call(
        give_kernel,
        out_shape=outs,
        in_specs=[anywhere] * 2 + [inside] * 7,
        out_specs=[inside] * 3,
        scratch_shapes=[
            pltpu.VMEM((count, dim), jnp.float32),
            pltpu.VMEM(d_own.shape, jnp.float32),
            pltpu.VMEM((slots, count, dim), bf16),
            pltpu.VMEM(top, bf16),
            pltpu.VMEM(top, bf16),
            pltpu.VMEM(left, bf16),
            pltpu.VMEM(left, bf16),
            pltpu.VMEM(w.shape, bf16),
            pltpu.VMEM((slots,) + x.shape[1:], bf16),
            pltpu.VMEM((slots, count, dim), bf16),
            pltpu.VMEM(corner, bf16),
            pltpu.VMEM(corner, bf16),
            pltpu.VMEM(top, bf16),
            pltpu.VMEM(top, bf16),
            dma((6,)),
            dma((6,)),
            dma((2,)),
        ]
        + [dma((slots,))] * 4,
        compiler_params=pltpu.CompilerParams(
            collective_id=1, has_side_effects=True, vmem_limit_bytes=VMEM_LIMIT
        ),
        name="give",
    )(w, d_own, x, *pieces)


def body(queries, keys, values, projection, d_outputs):
    f32, bf16 = jnp.float32, jnp.bfloat16
    q, k, v = queries[0], keys[0], values[0]
    frames, rows, cols, dim = q.shape
    tile_len = frames // 2
    query_count = frames * rows * cols
    depth = projection.shape[0]
    dp_count, dp_index = lax.axis_size("dp"), lax.axis_index("dp")

    *pieces, parts = fetch(k, v, d_outputs[0], projection)
    d_attended = jnp.zeros((query_count, dim), bf16)
    for step in range(dp_count):
        owner = lax.rem(dp_index + step, dp_count)
        d_attended = lax.dynamic_update_slice_in_dim(d_attended, parts[step], owner * depth, 1)

    bias = window_bias(tile_len, cols, TWIDE)
    attended, d_queries, d_own, *d_pieces = attention(bias, q, k, v, pieces, d_attended)

    sliced = []
    for step in range(dp_count):
        owner = lax.rem(dp_index + step, dp_count)
        sliced.append(lax.dynamic_slice_in_dim(attended, owner * depth, depth, 1))
    outputs, d_keys, d_values = give(jnp.stack(sliced), projection, d_own, d_pieces)
    return (outputs[None], d_queries[None], d_keys[None], d_values[None])


def solution(mesh):
    spread = P("dp", "tm", "height", None, None)
    in_specs = (spread, spread, spread, P("dp", None), spread)
    return jax.shard_map(
        body, mesh=mesh, in_specs=in_specs, out_specs=(spread,) * 4, check_vma=False
    )
```
